32 devices in a mesh: groups: 2 (over y), pool: 4 (over z), tensor: 4 (over x, core).
Axes of the slice: x: 2, y: 2, z: 4, core: 2. Of those that a mesh axis runs over, the one named last changes fastest.
Arguments:
- residual: bfloat16 [32, 8192], P('groups', 'pool'), parts along dimension 0, may hold values from -48 to 48
- norm_gain: bfloat16 [8192], P('pool'), may hold values from 0.099609375 to 1.8984375
- w_query: bfloat16 [8192, 8192], P('pool', 'tensor'), may hold values from -0.0625 to 0.0625
- w_key: bfloat16 [8192, 1024], P('pool', 'tensor'), may hold values from -0.0625 to 0.0625
- w_value: bfloat16 [8192, 1024], P('pool', 'tensor'), may hold values from -0.0625 to 0.0625
- w_out: bfloat16 [8192, 8192], P('tensor', 'pool'), may hold values from -0.0625 to 0.0625
- k_cache: bfloat16 [384, 128, 1024], P(('groups', 'pool'), None, 'tensor'), parts along dimension 0, may hold values from -210 to 210
- v_cache: bfloat16 [384, 128, 1024], P(('groups', 'pool'), None, 'tensor'), parts along dimension 0, may hold values from -6 to 6
- context_len: int32 [32], P('groups'), parts along dimension 0, may hold values from 0 to 6144, as said below
- routes: int32 [8, 4, 2], P('groups'), parts along dimension 0, may hold values from 0 to 15, as said below
- slot_route: int32 [384], P(('groups', 'pool')), parts along dimension 0, may hold values from -1 to 7, as said below
- slot_block: int32 [384], P(('groups', 'pool')), parts along dimension 0, may hold values from 0 to 47, as said below
Outputs:
- updated: bfloat16 [32, 8192], P('groups', 'pool'), parts along dimension 0
The draws below stay inside these ranges and needn't reach their ends.
There are 2 independent parts, one for each index of `groups`. The reference program is written for one: setup_inputs(seed, part) draws one part's arguments, and reference() takes and returns one part's arrays. A program takes and returns all parts, laid end to end along the dimension named above; an argument that names none is the same for every part. Nothing has to cross between parts.
Inputs may be any that keep to these rules, and one draw needn't show every extreme that they name: Request r has its home on pool device r // 4. routes[o, h] lists 2 distinct requests of home device h (h * 4 to h * 4 + 3); every request is listed for some owner. `slot_route`: slot g sits on pool device g // 48; -1 marks an empty slot, else e = h * 2 + c names the request routes[g // 48, h, c]. Each device has at most 48 live slots, and some device has all of them live. A listed request may have no block on that device. `slot_block`: the blocks of a request over all devices are numbered 0, 1, 2, ... without gaps or repeats; 0 in empty slots. No request has more than 48 blocks, and some request has exactly 48. A request's cached tokens are the positions block * 128 + i (i < 128) below context_len in its blocks; its last block holds at least one of them; a request without blocks has 0.
All inputs are finite; a program needn't handle non-finite values.
Results may differ from the reference program's by a relative error of at most 0.012.
The reference program's roundings to bfloat16 on the way count: a program that leaves them out, or rounds other values in their place, can miss the bound.
Values may be sent and summed in bfloat16 or wider, within the bound.
No kernel may reach another device: no remote copies, remote signals or barrier semaphores. Data moves between devices by JAX's collectives and lax.ppermute only.
A program may use at most 128 MiB of HBM per device.

```python
import math
import jax
import jax.numpy as jnp
from jax import lax

D = 8192
HEADS = 64
KV_HEADS = 8
HD = 128
BS = 128
SLOTS = 48
REQ_DEV = 4
CAP = 2
REQUESTS = 16
POOL_SLOTS = 192
N_POOL = 4


def draw_layout(key):
    key_route, key_owner, key_count, key_rank, key_pick, key_other, key_tail, key_busy = jax.random.split(key, 8)
    home_orders = jax.vmap(lambda subkey: jax.random.permutation(subkey, REQ_DEV))(jax.random.split(key_route, N_POOL))
    owner_order = jax.random.permutation(key_owner, N_POOL)
    owner_axis = jnp.arange(N_POOL)[:, None, None]
    home_axis = jnp.arange(N_POOL)[None, :, None]
    place_axis = jnp.arange(CAP)[None, None, :]
    list_place = (owner_order[owner_axis] * CAP + place_axis) % REQ_DEV
    routes = (home_axis * REQ_DEV + home_orders[home_axis, list_place]).astype(jnp.int32)
    live_count = jax.random.randint(key_count, (N_POOL,), 1, SLOTS + 1)
    busiest = jax.random.randint(key_busy, (), 0, N_POOL)
    device_ids = jnp.arange(N_POOL)
    live_count = jnp.where(device_ids == busiest, SLOTS, live_count)
    slot_ranks = jax.vmap(lambda subkey: jax.random.permutation(subkey, SLOTS))(jax.random.split(key_rank, N_POOL))
    live_slot = slot_ranks < live_count[:, None]
    first_pick = jax.random.randint(key_pick, (N_POOL, SLOTS), 0, N_POOL * CAP)
    second = jax.random.randint(key_other, (N_POOL, SLOTS), 0, N_POOL * CAP)
    on_busiest = (device_ids == busiest)[:, None]
    buffer_row = jnp.where(on_busiest, 0, jnp.minimum(first_pick, second))
    chosen = routes[device_ids[:, None], buffer_row // CAP, buffer_row % CAP]
    special = routes[busiest, 0, 0]
    live_slot = live_slot & (on_busiest | (chosen != special))
    first_request = jnp.where(live_slot, chosen, -1).reshape(-1)
    first_member = (first_request[:, None] == jnp.arange(REQUESTS)[None, :]).astype(jnp.int32)
    first_before = jnp.sum((jnp.cumsum(first_member, axis=0) - first_member) * first_member, axis=1)
    live_flat = live_slot.reshape(-1) & (first_before < SLOTS)
    chosen_flat = chosen.reshape(-1)
    slot_request = jnp.where(live_flat, chosen_flat, -1)
    slot_route = jnp.where(live_flat, buffer_row.reshape(-1), -1)
    member = (slot_request[:, None] == jnp.arange(REQUESTS)[None, :]).astype(jnp.int32)
    before = jnp.cumsum(member, axis=0) - member
    slot_block = jnp.sum(before * member, axis=1)
    block_count = jnp.sum(member, axis=0)
    short_tail = jax.random.randint(key_tail, (REQUESTS,), 0, BS)
    short_tail = jnp.where(jnp.arange(REQUESTS) == special, 0, short_tail)
    context_len = jnp.where(block_count > 0, block_count * BS - short_tail, 0)
    return (routes, slot_route.astype(jnp.int32), slot_block.astype(jnp.int32), context_len.astype(jnp.int32))


def draw_routes(key, part):
    return draw_layout(key)[0]


def draw_slot_route(key, part):
    return draw_layout(key)[1]


def draw_slot_block(key, part):
    return draw_layout(key)[2]


def draw_context_len(key, part):
    return draw_layout(key)[3]


def draw_residual(key, part):
    key = jax.random.fold_in(key, 11)
    key_base, key_row, key_column = jax.random.split(key, 3)
    array_shape = (REQUESTS, D)
    base_draw = jnp.clip(jax.random.normal(key_base, array_shape, jnp.float32), -6.0, 6.0)
    row_scale = jnp.exp(jax.random.uniform(key_row, (REQUESTS, 1), jnp.float32, 0.0, 2.3)) * 0.05
    column_ramp = jnp.exp(1.1 * jnp.arange(D, dtype=jnp.float32)[None, :] / D)
    column_scale = column_ramp * jnp.exp(jax.random.uniform(key_column, (1, D), jnp.float32, -1.15, 1.15))
    return (base_draw * row_scale * column_scale).astype(jnp.bfloat16)


def draw_k_cache(key, part):
    key = jax.random.fold_in(key, 13)
    key_base = jax.random.fold_in(key, 0)
    array_shape = (POOL_SLOTS, BS, KV_HEADS * HD)
    return (jnp.clip(jax.random.normal(key_base, array_shape, jnp.float32), -6.0, 6.0) * 1.5).astype(jnp.bfloat16)


def level_of(own_key, shape, pieces, low, high):
    loudness = 1.0
    for position, blocks in pieces:
        draws = jax.random.uniform(jax.random.fold_in(jax.random.fold_in(own_key, 6), position), (blocks,), jnp.float32, low / len(pieces), high / len(pieces))
        loudness = loudness * jnp.repeat(jnp.exp(draws), shape[position] // blocks).reshape((-1,) + (1,) * (len(shape) - 1 - position))
    return loudness


def normal_values(rng, shape, scale, bound, shards=(), kind=jnp.bfloat16):
    factor_of = level_of(rng, shape, shards, -0.22, 0.18) if shards else 1.0
    array = jax.random.normal(rng, shape, jnp.float32) * scale * factor_of
    return jnp.minimum(jnp.maximum(array, -bound), bound).astype(kind)


def setup_inputs(seed: int = 0, part: int = 0) -> dict:
    keys = jax.random.split(jax.random.key(seed), 13)
    part_splits = jax.random.split(jax.random.fold_in(keys[12], part), 13)
    return {
        "residual": draw_residual(jax.random.fold_in(jax.random.fold_in(keys[12], part), 71), part),
        "norm_gain": jnp.clip(1.0 + 0.18 * jax.random.normal(keys[1], (D,), jnp.float32), 0.099609375, 1.8984375).astype(jnp.bfloat16),
        "w_query": normal_values(keys[2], (D, HEADS * HD), D ** -0.5, 0.0625, ((0, 4), (1, 4))),
        "w_key": normal_values(keys[3], (D, KV_HEADS * HD), D ** -0.5, 0.0625, ((0, 4), (1, 4))),
        "w_value": normal_values(keys[4], (D, KV_HEADS * HD), D ** -0.5, 0.0625, ((0, 4), (1, 4))),
        "w_out": normal_values(keys[5], (HEADS * HD, D), (HEADS * HD) ** -0.5, 0.0625, ((0, 4), (1, 4))),
        "k_cache": draw_k_cache(jax.random.fold_in(jax.random.fold_in(keys[12], part), 71), part),
        "v_cache": normal_values(part_splits[7], (POOL_SLOTS, BS, KV_HEADS * HD), 1.0, 6.0, ((0, 4), (2, 4))),
        "context_len": draw_context_len(jax.random.fold_in(jax.random.fold_in(keys[12], part), 71), part),
        "routes": draw_routes(jax.random.fold_in(jax.random.fold_in(keys[12], part), 71), part),
        "slot_route": draw_slot_route(jax.random.fold_in(jax.random.fold_in(keys[12], part), 71), part),
        "slot_block": draw_slot_block(jax.random.fold_in(jax.random.fold_in(keys[12], part), 71), part),
    }


EPSILON = 1e-05
THETA = 500000.0
NEG_FILL = -1e+30
EXACT = lax.Precision.HIGHEST

def rotate(vectors, positions):
    half_dim = vectors.shape[-1] // 2
    frequencies = THETA ** (-2.0 * jnp.arange(half_dim, dtype=jnp.float32) / vectors.shape[-1])
    angles = positions.astype(jnp.float32)[:, None] * frequencies[None, :]
    cosine = jnp.cos(angles)[:, None, :]
    sine_part = jnp.sin(angles)[:, None, :]
    first_half = vectors[..., :half_dim]
    second_half = vectors[..., half_dim:]
    return jnp.concatenate([first_half * cosine - second_half * sine_part, second_half * cosine + first_half * sine_part], axis=-1)

def reference(residual, norm_gain, w_query, w_key, w_value, w_out, k_cache, v_cache, context_len, routes, slot_route, slot_block):
    group_size = HEADS // KV_HEADS
    score_scale = 1.0 / math.sqrt(HD)
    resid_f = residual.astype(jnp.float32)
    meansq = lax.optimization_barrier(jnp.mean(resid_f * resid_f, axis=1, keepdims=True))
    normed = (resid_f * lax.rsqrt(meansq + EPSILON) * norm_gain.astype(jnp.float32)[None, :]).astype(jnp.bfloat16)
    query_raw = jnp.dot(normed, w_query, preferred_element_type=jnp.float32).reshape(REQUESTS, HEADS, HD)
    key_raw = jnp.dot(normed, w_key, preferred_element_type=jnp.float32).reshape(REQUESTS, KV_HEADS, HD)
    value_new = jnp.dot(normed, w_value, preferred_element_type=jnp.float32).astype(jnp.bfloat16).reshape(REQUESTS, KV_HEADS, HD)
    query = rotate(query_raw, context_len).astype(jnp.bfloat16).reshape(REQUESTS, KV_HEADS, group_size, HD)
    key_new = rotate(key_raw, context_len).astype(jnp.bfloat16)
    owner_of = jnp.arange(POOL_SLOTS, dtype=jnp.int32) // SLOTS
    safe_entry = jnp.maximum(slot_route, 0)
    slot_request = jnp.where(slot_route >= 0, routes[owner_of, safe_entry // CAP, safe_entry % CAP], -1).astype(jnp.int32)

    def device_stats(operands):
        requests_here, blocks_here, keys_here, values_here = operands
        safe_ids = jnp.maximum(requests_here, 0)
        slot_query = query[safe_ids].astype(jnp.float32)
        slot_len = jnp.where(requests_here >= 0, context_len[safe_ids], 0)
        positions = blocks_here[:, None] * BS + jnp.arange(BS, dtype=jnp.int32)[None, :]
        valid_mask = (positions < slot_len[:, None])[:, None, None, :]
        key_grid = keys_here.astype(jnp.float32).reshape(SLOTS, BS, KV_HEADS, HD)
        value_grid = values_here.astype(jnp.float32).reshape(SLOTS, BS, KV_HEADS, HD)
        scores = jnp.einsum('skgd,sbkd->skgb', slot_query, key_grid, precision=EXACT) * score_scale
        block_peak = lax.optimization_barrier(jnp.max(jnp.where(valid_mask, scores, NEG_FILL), axis=3))
        exponent = jnp.exp(jnp.where(valid_mask, scores - block_peak[..., None], NEG_FILL))
        weights = exponent.astype(jnp.bfloat16).astype(jnp.float32)
        block_sum = jnp.einsum('skgb,sbkd->skgd', weights, value_grid, precision=EXACT)
        return (block_peak, lax.optimization_barrier(jnp.sum(exponent, axis=3)), block_sum)
    peaks, masses, sums = lax.map(device_stats, (slot_request.reshape(N_POOL, SLOTS), slot_block.reshape(N_POOL, SLOTS), k_cache.reshape(N_POOL, SLOTS, BS, KV_HEADS * HD), v_cache.reshape(N_POOL, SLOTS, BS, KV_HEADS * HD)))
    peaks = peaks.reshape(POOL_SLOTS, KV_HEADS, group_size)
    masses = masses.reshape(POOL_SLOTS, KV_HEADS, group_size)
    sums = sums.reshape(POOL_SLOTS, KV_HEADS, group_size, HD)
    own = jnp.einsum('rkgd,rkd->rkg', query.astype(jnp.float32), key_new.astype(jnp.float32), precision=EXACT) * score_scale
    member = slot_request[:, None] == jnp.arange(REQUESTS, dtype=jnp.int32)[None, :]
    best = jnp.maximum(own, lax.optimization_barrier(jnp.max(jnp.where(member[:, :, None, None], peaks[:, None], NEG_FILL), axis=0)))
    safe_all = jnp.maximum(slot_request, 0)
    factor = jnp.where((slot_request >= 0)[:, None, None], jnp.exp(peaks - best[safe_all]), 0.0)
    numerator = jax.ops.segment_sum(factor[..., None] * sums, safe_all, num_segments=REQUESTS)
    denominator = jax.ops.segment_sum(factor * masses, safe_all, num_segments=REQUESTS)
    own_weight = jnp.exp(own - best)
    numerator = numerator + own_weight[..., None] * value_new.astype(jnp.float32)[:, :, None, :]
    denominator = denominator + own_weight
    attention = (numerator / denominator[..., None]).astype(jnp.bfloat16).reshape(REQUESTS, HEADS * HD)
    updated = resid_f + jnp.dot(attention, w_out, preferred_element_type=jnp.float32)
    return updated.astype(jnp.bfloat16)
```

```python
import functools
import math

import jax
import jax.numpy as jnp
from jax import lax
from jax.experimental import pallas as pl
from jax.experimental.pallas import tpu as pltpu
from jax.sharding import PartitionSpec as P

D = 8192
HD = 128
BS = 128

EPSILON = 1e-05
THETA = 500000.0
NEG_FILL = -1e30
EXACT = lax.Precision.HIGHEST
CHUNK = 256


def listed_at(routes, owner, row):
    per_home = routes.shape[1]
    return routes[owner, row % per_home, row // per_home]


def load_kernel(count, *rest):
    sources, outs, sems = rest[1 : 1 + count], rest[1 + count : -1], rest[-1]
    copies = [
        pltpu.make_async_copy(sources[i], outs[i], sems.at[i]) for i in range(count)
    ]
    for copy in copies:
        copy.start()
    for copy in copies:
        copy.wait()


def load(after, *sources):
    count = len(sources)
    return pl.pallas_call(
        functools.partial(load_kernel, count),
        out_shape=[pltpu.VMEM(source.shape, source.dtype) for source in sources],
        in_specs=[pl.BlockSpec(memory_space=pl.ANY)] * (count + 1),
        out_specs=[pl.BlockSpec(memory_space=pltpu.VMEM)] * count,
        scratch_shapes=[pltpu.SemaphoreType.DMA((count,))],
        compiler_params=pltpu.CompilerParams(vmem_limit_bytes=4 * 2**20),
        cost_estimate=pl.CostEstimate(
            flops=0,
            bytes_accessed=sum(source.size * source.dtype.itemsize for source in sources),
            transcendentals=0,
        ),
        name="load",
    )(after, *[pltpu.with_memory_space_constraint(source, pltpu.HBM) for source in sources])


def square_kernel(residual, out):
    resid_f = residual[...].astype(jnp.float32)
    out[...] = jnp.broadcast_to(
        jnp.sum(resid_f * resid_f, axis=1, keepdims=True), out.shape
    )


def project_kernel(pool_count, routes, residual, gain, *rest):
    squares, rest = rest[:pool_count], rest[pool_count:]
    weights, outs = rest[:3], rest[3:]
    listed = outs[0].shape[0]
    requests = residual.shape[0]
    rows = pool_count * listed
    me = lax.axis_index("pool")
    total = squares[0][...]
    for part in squares[1:]:
        total = total + part[...]
    scale = lax.rsqrt(total[:, :1] / D + EPSILON)
    resid_f = residual[...].astype(jnp.float32)
    normed = resid_f * scale * gain[...].astype(jnp.float32)[None, :]
    row_ids = lax.broadcasted_iota(jnp.int32, (rows, requests), 0)
    column_ids = lax.broadcasted_iota(jnp.int32, (rows, requests), 1)
    wanted = jnp.zeros((rows, requests), jnp.int32)
    for shift in range(pool_count):
        owner = lax.rem(me + shift, pool_count)
        for row in range(listed):
            wanted = jnp.where(
                row_ids == shift * listed + row, listed_at(routes, owner, row), wanted
            )
    pick = (column_ids == wanted).astype(jnp.float32).astype(jnp.bfloat16)
    picked = jnp.dot(
        pick, normed.astype(jnp.bfloat16), preferred_element_type=jnp.float32
    ).astype(jnp.bfloat16)
    place = 0
    for source in weights:
        for first in range(0, source.shape[1], CHUNK):
            product = jnp.dot(
                picked, source[:, first : first + CHUNK], preferred_element_type=jnp.float32
            )
            for shift in range(pool_count):
                outs[shift][:, place : place + CHUNK] = product[
                    shift * listed : (shift + 1) * listed
                ]
            place += CHUNK


def attend_kernel(
    pool_count, local_kv, group, routes, context_len, slot_route, slot_block, turn, *rest
):
    parts, (keys, values, out) = rest[:pool_count], rest[pool_count : pool_count + 3]
    turned, flat_query, flat_own, query, score, peak, mass, total = rest[pool_count + 3 :]
    listed = parts[0].shape[0]
    heads = local_kv * group
    slots = keys.shape[0]
    key_width = local_kv * HD
    homes = pool_count
    per_home = listed // homes
    score_scale = 1.0 / math.sqrt(HD)
    me = lax.axis_index("pool")
    for row in range(listed):
        turned[row : row + 1, :] = turn[pl.ds(listed_at(routes, me, row), 1), :]
    cosine, sine = turned[:, :HD], turned[:, HD:]

    def column(first):
        value = parts[0][:, first : first + HD]
        for part in parts[1:]:
            value = value + part[:, first : first + HD]
        return value

    def rotated(first):
        vector = column(first)
        vector = vector * cosine + pltpu.roll(vector, HD // 2, 1) * sine
        return vector.astype(jnp.bfloat16).astype(jnp.float32)

    new_keys = [rotated(k * HD) for k in range(local_kv)]
    new_values = [
        column(key_width + k * HD).astype(jnp.bfloat16).astype(jnp.float32)
        for k in range(local_kv)
    ]
    for head in range(heads):
        vector = rotated(2 * key_width + head * HD)
        own = jnp.sum(vector * new_keys[head // group], axis=1, keepdims=True) * score_scale
        flat_query[head * listed : (head + 1) * listed, :] = vector
        flat_own[head * listed : (head + 1) * listed, :] = jnp.broadcast_to(own, (listed, HD))
    lanes = lax.broadcasted_iota(jnp.int32, (heads, HD), 1)
    head_kv = lax.broadcasted_iota(jnp.int32, (heads, HD), 0) // group

    owns, mine = [], []
    for row in range(listed):
        home = row // per_home
        request = listed_at(routes, me, row)
        taken = jnp.int32(0)
        for owner in range(pool_count):
            for place in range(per_home):
                same = routes[owner, place, home] == request
                taken = taken | ((owner < me) & same).astype(jnp.int32)
        vector = flat_query[pl.ds(row, heads, stride=listed), :]
        query[row] = jnp.concatenate(
            [jnp.where(head_kv == k, vector, 0.0) for k in range(local_kv)], axis=1
        ).astype(jnp.bfloat16)
        own = flat_own[pl.ds(row, heads, stride=listed), :]
        own = jnp.where(taken == 0, own, NEG_FILL)
        owns.append(own)
        mine.append(taken == 0)
        peak[row] = own

    def slot_of(slot):
        entry = slot_route[slot]
        row = jnp.maximum(entry, 0)
        length = jnp.where(entry >= 0, context_len[listed_at(routes, me, row)], 0)
        return row, length - slot_block[slot] * BS

    for slot in range(slots):
        row, limit = slot_of(slot)
        value = (
            lax.dot_general(
                query[row],
                keys[slot],
                (((1,), (1,)), ((), ())),
                preferred_element_type=jnp.float32,
            )
            * score_scale
        )
        value = jnp.where(lanes < limit, value, NEG_FILL)
        score[slot] = value
        peak[row] = jnp.maximum(peak[row], value)
    for row in range(listed):
        top = jnp.broadcast_to(jnp.max(peak[row], axis=1, keepdims=True), (heads, HD))
        peak[row] = top
        weight = jnp.where(mine[row], jnp.exp(owns[row] - top), 0.0)
        mass[row] = jnp.where(lanes == 0, weight, 0.0)
        fresh = jnp.zeros((heads, HD), jnp.float32)
        for k in range(local_kv):
            fresh = jnp.where(
                head_kv == k, jnp.broadcast_to(new_values[k][row : row + 1], (heads, HD)), fresh
            )
        total[row] = weight * fresh
    for slot in range(slots):
        row, limit = slot_of(slot)
        expo = jnp.where(lanes < limit, jnp.exp(score[slot] - peak[row]), 0.0)
        mass[row] += expo
        wide = jnp.dot(
            expo.astype(jnp.bfloat16), values[slot], preferred_element_type=jnp.float32
        )
        product = wide[:, :HD]
        for k in range(1, local_kv):
            product = jnp.where(head_kv == k, wide[:, k * HD : (k + 1) * HD], product)
        total[row] += product
    stats = jnp.zeros((heads, HD), jnp.float32)
    for row in range(listed):
        row_mass = jnp.sum(mass[row], axis=1, keepdims=True)
        row_peak = peak[row]
        out[row] = jnp.where(
            row_mass > 0.0, total[row] / jnp.where(row_mass > 0.0, row_mass, 1.0), 0.0
        ).astype(jnp.bfloat16)
        for first, left in ((0, row_peak), (3, row_mass)):
            for piece in range(first, first + 3):
                part = left.astype(jnp.bfloat16).astype(jnp.float32)
                stats = jnp.where(lanes == piece * listed + row, part, stats)
                left = left - part
    out[listed] = stats.astype(jnp.bfloat16)


def merge_kernel(pool_count, routes, *rest):
    parts, (w_out, out) = rest[:pool_count], rest[pool_count : pool_count + 2]
    best, numerator, denominator, flat = rest[pool_count + 2 :]
    listed = parts[0].shape[0] - 1
    requests, heads = best.shape[:2]
    me = lax.axis_index("pool")
    best[...] = jnp.full(best.shape, NEG_FILL, jnp.float32)
    numerator[...] = jnp.zeros_like(numerator)
    denominator[...] = jnp.zeros_like(denominator)
    entries = []
    for shift in range(pool_count):
        owner = lax.rem(me + pool_count - shift, pool_count)
        stats = parts[shift][listed].astype(jnp.float32)
        for row in range(listed):
            request = listed_at(routes, owner, row)
            pieces = [
                stats[:, piece * listed + row : piece * listed + row + 1] for piece in range(6)
            ]
            peak = jnp.broadcast_to(pieces[0] + pieces[1] + pieces[2], (heads, HD))
            mass = jnp.broadcast_to(pieces[3] + pieces[4] + pieces[5], (heads, HD))
            entries.append((shift, row, request, peak, mass))
            best[request] = jnp.maximum(best[request], peak)
    for shift, row, request, peak, mass in entries:
        weight = jnp.exp(peak - best[request]) * mass
        numerator[request] += weight * parts[shift][row].astype(jnp.float32)
        denominator[request] += weight
    for request in range(requests):
        flat[request * heads : (request + 1) * heads, :] = (
            numerator[request] / denominator[request]
        )
    attention = jnp.concatenate(
        [flat[pl.ds(head, requests, stride=heads), :].astype(jnp.bfloat16) for head in range(heads)],
        axis=1,
    )
    for first in range(0, out.shape[1], CHUNK):
        out[:, first : first + CHUNK] = jnp.dot(
            attention, w_out[:, first : first + CHUNK], preferred_element_type=jnp.float32
        )


def spread(value, axis):
    count = lax.axis_size(axis)
    return [value] + [
        lax.ppermute(value, axis, [(i, (i + shift) % count) for i in range(count)])
        for shift in range(1, count)
    ]


def pin(value):
    return pltpu.with_memory_space_constraint(value, pltpu.VMEM)


def close_pool(
    residual,
    norm_gain,
    w_query,
    w_key,
    w_value,
    w_out,
    k_cache,
    v_cache,
    context_len,
    routes,
    slot_route,
    slot_block,
):
    pool_count = lax.axis_size("pool")
    requests, depth = residual.shape
    query_width, key_width = w_query.shape[1], w_key.shape[1]
    heads, local_kv = query_width // HD, key_width // HD
    group = heads // local_kv
    listed = routes.shape[1] * routes.shape[2]
    slots = k_cache.shape[0]
    width = query_width + 2 * key_width
    routes = routes.transpose(0, 2, 1)
    in_smem = pl.BlockSpec(memory_space=pltpu.SMEM)
    in_vmem = pl.BlockSpec(memory_space=pltpu.VMEM)
    f32 = jnp.float32
    spell = pl.CostEstimate(flops=0, bytes_accessed=2**25, transcendentals=0)

    squares = pl.pallas_call(
        square_kernel,
        out_shape=jax.ShapeDtypeStruct((requests, HD), f32),
        in_specs=[in_vmem],
        out_specs=in_vmem,
        compiler_params=pltpu.CompilerParams(vmem_limit_bytes=4 * 2**20),
        cost_estimate=spell,
        name="square",
    )(residual)
    near_key, near_value, near_query = load(squares, w_key, w_value, w_query)
    sent = pl.pallas_call(
        functools.partial(project_kernel, pool_count),
        out_shape=[jax.ShapeDtypeStruct((listed, width), f32)] * pool_count,
        in_specs=[in_smem] + [in_vmem] * (pool_count + 5),
        out_specs=[in_vmem] * pool_count,
        compiler_params=pltpu.CompilerParams(vmem_limit_bytes=8 * 2**20),
        cost_estimate=spell,
        name="project",
    )(
        routes,
        residual,
        norm_gain,
        *spread(squares, "pool"),
        pin(near_key),
        pin(near_value),
        pin(near_query),
    )
    received = [sent[0]] + [
        lax.ppermute(sent[s], "pool", [(i, (i + s) % pool_count) for i in range(pool_count)])
        for s in range(1, pool_count)
    ]

    frequencies = THETA ** (-2.0 * jnp.arange(HD // 2, dtype=f32) / HD)
    angles = context_len.astype(f32)[:, None] * frequencies[None, :]
    cosine, sine = jnp.cos(angles), jnp.sin(angles)
    turn = jnp.concatenate([cosine, cosine, -sine, sine], axis=1)
    near_k, near_v = load(sent[0], k_cache, v_cache)
    partial = pl.pallas_call(
        functools.partial(attend_kernel, pool_count, local_kv, group),
        out_shape=jax.ShapeDtypeStruct((listed + 1, heads, HD), jnp.bfloat16),
        in_specs=[in_smem] * 4 + [in_vmem] * (pool_count + 3),
        out_specs=in_vmem,
        scratch_shapes=[
            pltpu.VMEM((listed, 2 * HD), f32),
            pltpu.VMEM((heads * listed, HD), f32),
            pltpu.VMEM((heads * listed, HD), f32),
            pltpu.VMEM((listed, heads, key_width), jnp.bfloat16),
            pltpu.VMEM((slots, heads, HD), f32),
            pltpu.VMEM((listed, heads, HD), f32),
            pltpu.VMEM((listed, heads, HD), f32),
            pltpu.VMEM((listed, heads, HD), f32),
        ],
        compiler_params=pltpu.CompilerParams(vmem_limit_bytes=8 * 2**20),
        cost_estimate=spell,
        name="attend",
    )(routes, context_len, slot_route, slot_block, turn, *received, pin(near_k), pin(near_v))
    partials = spread(partial, "pool")
    (near_out,) = load(partial, w_out)

    product = pl.pallas_call(
        functools.partial(merge_kernel, pool_count),
        out_shape=jax.ShapeDtypeStruct((requests, w_out.shape[1]), f32),
        in_specs=[in_smem] + [in_vmem] * (pool_count + 1),
        out_specs=in_vmem,
        scratch_shapes=[
            pltpu.VMEM((requests, heads, HD), f32),
            pltpu.VMEM((requests, heads, HD), f32),
            pltpu.VMEM((requests, heads, HD), f32),
            pltpu.VMEM((requests * heads, HD), f32),
        ],
        compiler_params=pltpu.CompilerParams(vmem_limit_bytes=8 * 2**20),
        cost_estimate=spell,
        name="merge",
    )(routes, *partials, pin(near_out))
    tensor_count = lax.axis_size("tensor")
    distance = 1
    while distance < tensor_count:
        product = product + lax.ppermute(
            product, "tensor", [(i, i ^ distance) for i in range(tensor_count)]
        )
        distance *= 2
    return (residual.astype(f32) + product).astype(jnp.bfloat16)


def rotate(vectors, positions):
    half_dim = vectors.shape[-1] // 2
    frequencies = THETA ** (-2.0 * jnp.arange(half_dim, dtype=jnp.float32) / vectors.shape[-1])
    angles = positions.astype(jnp.float32)[:, None] * frequencies[None, :]
    cosine = jnp.cos(angles)[:, None, :]
    sine_part = jnp.sin(angles)[:, None, :]
    first_half = vectors[..., :half_dim]
    second_half = vectors[..., half_dim:]
    return jnp.concatenate(
        [
            first_half * cosine - second_half * sine_part,
            second_half * cosine + first_half * sine_part,
        ],
        axis=-1,
    )


def send_back(parts):
    return (
        lax.all_to_all(parts[0], "pool", split_axis=0, concat_axis=0, tiled=True),
        lax.all_to_all(parts[1], "pool", split_axis=0, concat_axis=0, tiled=True),
        lax.all_to_all(parts[2], "pool", split_axis=0, concat_axis=0, tiled=True),
    )


def wide_pool(
    residual,
    norm_gain,
    w_query,
    w_key,
    w_value,
    w_out,
    k_cache,
    v_cache,
    context_len,
    routes,
    slot_route,
    slot_block,
):
    pool_count = lax.axis_size("pool")
    pool_index = lax.axis_index("pool")
    request_count = residual.shape[0]
    per_home = request_count // pool_count
    home_first = pool_index * per_home
    query_width = w_query.shape[1]
    key_width = w_key.shape[1]
    local_heads = query_width // HD
    local_kv = key_width // HD
    group_size = local_heads // local_kv
    slot_count = k_cache.shape[0]
    score_scale = 1.0 / math.sqrt(HD)
    resid_f = residual.astype(jnp.float32)
    square_total = lax.psum(jnp.sum(resid_f * resid_f, axis=1), "pool")
    normed = (
        resid_f
        * lax.rsqrt(square_total / D + EPSILON)[:, None]
        * norm_gain.astype(jnp.float32)[None, :]
    ).astype(jnp.bfloat16)
    owner_routes = lax.dynamic_slice_in_dim(routes, pool_index, 1, 0)[0].reshape(-1)
    slot_request = jnp.where(slot_route >= 0, owner_routes[jnp.maximum(slot_route, 0)], -1)
    key_blocks = k_cache.reshape(slot_count, BS, local_kv, HD)
    value_blocks = v_cache.reshape(slot_count, BS, local_kv, HD)
    positions = slot_block[:, None] * BS + jnp.arange(BS, dtype=jnp.int32)[None, :]
    sent_ids = lax.dynamic_slice_in_dim(routes, pool_index, 1, 1)[:, 0, :]
    home_rows = lax.psum_scatter(
        jnp.concatenate(
            [
                jnp.dot(normed, w_query, preferred_element_type=jnp.float32),
                jnp.dot(normed, w_key, preferred_element_type=jnp.float32),
                jnp.dot(normed, w_value, preferred_element_type=jnp.float32),
            ],
            axis=1,
        ),
        "pool",
        scatter_dimension=0,
        tiled=True,
    )
    home_len = lax.dynamic_slice_in_dim(context_len, home_first, per_home, 0)
    row_total = home_rows.shape[0]
    query = rotate(home_rows[:, :query_width].reshape(row_total, local_heads, HD), home_len).astype(
        jnp.bfloat16
    )
    key_new = rotate(
        home_rows[:, query_width : query_width + key_width].reshape(row_total, local_kv, HD),
        home_len,
    ).astype(jnp.bfloat16)
    value_new = (
        home_rows[:, query_width + key_width :]
        .astype(jnp.bfloat16)
        .reshape(row_total, local_kv, HD)
    )
    home_query = query.reshape(row_total, query_width)
    sent_query = home_query[sent_ids - home_first]
    sent_info = jnp.stack([sent_ids, context_len[sent_ids]], axis=-1)
    rows_query = lax.all_to_all(sent_query, "pool", split_axis=0, concat_axis=0, tiled=True)
    rows_info = lax.all_to_all(sent_info, "pool", split_axis=0, concat_axis=0, tiled=True)
    home_total = rows_query.shape[0]
    item_total = rows_query.shape[1]
    flat_query = rows_query.reshape(home_total * item_total, query_width)
    flat_ids = rows_info[..., 0].reshape(-1)
    flat_len = rows_info[..., 1].reshape(-1)
    matches = slot_request[:, None] == flat_ids[None, :]
    slot_query = jnp.dot(
        matches.astype(jnp.bfloat16), flat_query, preferred_element_type=jnp.float32
    ).astype(jnp.bfloat16)
    grouped = slot_query.reshape(slot_count, local_kv, group_size, HD)
    slot_len = jnp.sum(jnp.where(matches, flat_len[None, :], 0), axis=1)
    present = jnp.any(matches, axis=1)
    in_range = present[:, None] & (positions < slot_len[:, None])
    valid_mask = in_range[:, None, None, :]
    scores = (
        jnp.einsum("skgd,sbkd->skgb", grouped, key_blocks, preferred_element_type=jnp.float32)
        * score_scale
    )
    block_peak = jnp.max(jnp.where(valid_mask, scores, NEG_FILL), axis=3)
    exponent = jnp.exp(jnp.where(valid_mask, scores - block_peak[..., None], NEG_FILL))
    weights = exponent.astype(jnp.bfloat16)
    block_sum = jnp.einsum(
        "skgb,sbkd->skgd", weights, value_blocks, preferred_element_type=jnp.float32
    )
    block_mass = jnp.sum(exponent, axis=3)
    hits = matches.T
    row_peak = jnp.max(jnp.where(hits[:, :, None, None], block_peak[None], NEG_FILL), axis=1)
    factor = jnp.where(hits[:, :, None, None], jnp.exp(block_peak[None] - row_peak[:, None]), 0.0)
    row_sum = jnp.einsum("rskg,skgd->rkgd", factor, block_sum, precision=EXACT)
    row_mass = jnp.einsum("rskg,skg->rkg", factor, block_mass, precision=EXACT)
    back_sum, back_peak, back_mass = send_back(
        (
            row_sum.reshape(home_total, item_total, query_width),
            row_peak.reshape(home_total, item_total, local_heads),
            row_mass.reshape(home_total, item_total, local_heads),
        )
    )
    local_ids = (sent_ids - home_first).reshape(-1)
    owned = local_ids[:, None] == jnp.arange(per_home, dtype=jnp.int32)[None, :]
    sum_rows = back_sum.reshape(-1, local_kv, group_size, HD)
    peak_rows = back_peak.reshape(-1, local_kv, group_size)
    mass_rows = back_mass.reshape(-1, local_kv, group_size)
    query_grid = home_query.reshape(per_home, local_kv, group_size, HD)
    own_score = (
        jnp.einsum("rkgd,rkd->rkg", query_grid, key_new, preferred_element_type=jnp.float32)
        * score_scale
    )
    overall = jnp.maximum(
        own_score, jnp.max(jnp.where(owned[:, :, None, None], peak_rows[:, None], NEG_FILL), axis=0)
    )
    merge_weight = jnp.where(
        owned[:, :, None, None], jnp.exp(peak_rows[:, None] - overall[None]), 0.0
    )
    own_weight = jnp.exp(own_score - overall)
    numerator = (
        jnp.einsum("prkg,pkgd->rkgd", merge_weight, sum_rows, precision=EXACT)
        + own_weight[..., None] * value_new.astype(jnp.float32)[:, :, None, :]
    )
    denominator = jnp.einsum("prkg,pkg->rkg", merge_weight, mass_rows, precision=EXACT) + own_weight
    attention = (
        (numerator / denominator[..., None]).astype(jnp.bfloat16).reshape(per_home, query_width)
    )
    partial_out = jnp.dot(
        lax.all_gather(attention, "pool", axis=0, tiled=True),
        w_out,
        preferred_element_type=jnp.float32,
    )
    head_total = lax.psum(partial_out, "tensor")
    return (resid_f + head_total).astype(jnp.bfloat16)


def solution(mesh):
    placed = (
        P("groups", "pool"),
        P("pool"),
        P("pool", "tensor"),
        P("pool", "tensor"),
        P("pool", "tensor"),
        P("tensor", "pool"),
        P(("groups", "pool"), None, "tensor"),
        P(("groups", "pool"), None, "tensor"),
        P("groups"),
        P("groups", None, None),
        P(("groups", "pool")),
        P(("groups", "pool")),
    )
    pool_count, tensor_count = mesh.shape["pool"], mesh.shape["tensor"]
    close = pool_count <= 4 and tensor_count & (tensor_count - 1) == 0
    return jax.shard_map(
        close_pool if close else wide_pool,
        mesh=mesh,
        in_specs=placed,
        out_specs=P("groups", "pool"),
        check_vma=False,
    )
```

```python
import functools
import math

import jax
import jax.numpy as jnp
from jax import lax
from jax.experimental import pallas as pl
from jax.experimental.pallas import tpu as pltpu
from jax.sharding import PartitionSpec as P

D = 8192
HD = 128
BS = 128

EPSILON = 1e-05
THETA = 500000.0
NEG_FILL = -1e30
EXACT = lax.Precision.HIGHEST
CHUNK = 256
GROW = 128.0


def listed_at(routes, owner, row):
    per_home = routes.shape[1]
    return routes[owner, row % per_home, row // per_home]


def load_kernel(count, *rest):
    sources, outs, sems = rest[1 : 1 + count], rest[1 + count : -1], rest[-1]
    copies = []
    for source, out, place in zip(sources, outs, range(count)):
        copies.append(pltpu.make_async_copy(leading(source, out), out, sems.at[place]))
    for copy in copies:
        copy.start()
    for copy in copies:
        copy.wait()


def start_first(copies):
    @pl.when(lax.axis_index("pool") >= 0)
    def _():
        for copy in copies:
            copy.start()


def leading(source, out):
    return source.at[pl.ds(0, out.shape[0])]


def load(after, *sources):
    count = len(sources)
    shapes = [(rows,) + source.shape[1:] for source, rows in sources]
    return pl.pallas_call(
        functools.partial(load_kernel, count),
        out_shape=[pltpu.VMEM(shape, jnp.bfloat16) for shape in shapes],
        in_specs=[pl.BlockSpec(memory_space=pl.ANY)] * (count + 1),
        out_specs=[pl.BlockSpec(memory_space=pltpu.VMEM)] * count,
        scratch_shapes=[pltpu.SemaphoreType.DMA((count,))],
        compiler_params=pltpu.CompilerParams(vmem_limit_bytes=4 * 2**20),
        cost_estimate=pl.CostEstimate(
            flops=0,
            bytes_accessed=sum(2 * math.prod(shape) for shape in shapes),
            transcendentals=0,
        ),
        name="load",
    )(after, *[in_hbm(source) for source, _ in sources])


def square_kernel(residual, out):
    resid_f = residual[...].astype(jnp.float32)
    out[...] = jnp.broadcast_to(
        jnp.sum(resid_f * resid_f, axis=1, keepdims=True), out.shape
    )


def project_kernel(pool_count, routes, residual, gain, *rest):
    squares, rest = rest[:pool_count], rest[pool_count:]
    weights, source, outs, (late, sems) = rest[:3], rest[3], rest[4:-2], rest[-2:]
    early = weights[-1].shape[0]
    copies = []
    for place in range(late.shape[0]):
        depths = pl.ds(early + place * CHUNK, CHUNK)
        copies.append(pltpu.make_async_copy(source.at[depths], late.at[place], sems.at[place]))
    start_first(copies)
    listed = outs[0].shape[0]
    requests = residual.shape[0]
    rows = pool_count * listed
    me = lax.axis_index("pool")
    total = squares[0][...]
    for part in squares[1:]:
        total = total + part[...]
    scale = lax.rsqrt(total[:, :1] / D + EPSILON)
    resid_f = residual[...].astype(jnp.float32)
    normed = resid_f * scale * gain[...].astype(jnp.float32)[None, :]
    row_ids = lax.broadcasted_iota(jnp.int32, (rows, requests), 0)
    column_ids = lax.broadcasted_iota(jnp.int32, (rows, requests), 1)
    wanted = jnp.zeros((rows, requests), jnp.int32)
    for shift in range(pool_count):
        owner = lax.rem(me + shift, pool_count)
        for row in range(listed):
            wanted = jnp.where(
                row_ids == shift * listed + row, listed_at(routes, owner, row), wanted
            )
    pick = (column_ids == wanted).astype(jnp.float32).astype(jnp.bfloat16)
    picked = jnp.dot(
        pick, normed.astype(jnp.bfloat16), preferred_element_type=jnp.float32
    ).astype(jnp.bfloat16)
    place = 0
    for weight in weights:
        for first in range(0, weight.shape[1], CHUNK):
            product = jnp.dot(
                picked[:, : weight.shape[0]],
                weight[:, first : first + CHUNK],
                preferred_element_type=jnp.float32,
            )
            for shift in range(pool_count):
                outs[shift][:, place + first : place + first + CHUNK] = product[
                    shift * listed : (shift + 1) * listed
                ]
        place += weight.shape[1]
    place -= weights[-1].shape[1]
    for block, copy in enumerate(copies):
        depths = slice(early + block * CHUNK, early + (block + 1) * CHUNK)
        copy.wait()
        for first in range(0, late.shape[2], CHUNK):
            product = jnp.dot(
                picked[:, depths],
                late[block, :, first : first + CHUNK],
                preferred_element_type=jnp.float32,
            )
            for shift in range(pool_count):
                outs[shift][:, place + first : place + first + CHUNK] += product[
                    shift * listed : (shift + 1) * listed
                ]


def attend_kernel(
    pool_count, local_kv, group, routes, context_len, slot_route, slot_block, turn, *rest
):
    parts, (keys, values, out) = rest[:pool_count], rest[pool_count : pool_count + 3]
    turned, flat_query, flat_own, query, score, peak, mass, total = rest[pool_count + 3 :]
    listed = parts[0].shape[0]
    heads = local_kv * group
    slots = keys.shape[0]
    key_width = local_kv * HD
    homes = pool_count
    per_home = listed // homes
    score_scale = 1.0 / math.sqrt(HD)
    me = lax.axis_index("pool")
    for row in range(listed):
        turned[row : row + 1, :] = turn[pl.ds(listed_at(routes, me, row), 1), :]
    cosine, sine = turned[:, :HD], turned[:, HD:]

    def column(first):
        value = parts[1][:, first : first + HD]
        for part in parts[2:]:
            value = value + part[:, first : first + HD]
        return parts[0][:, first : first + HD] + value * (1.0 / GROW)

    def rotated(first):
        vector = column(first)
        vector = vector * cosine + pltpu.roll(vector, HD // 2, 1) * sine
        return vector.astype(jnp.bfloat16).astype(jnp.float32)

    new_keys = [rotated(k * HD) for k in range(local_kv)]
    new_values = [
        column(key_width + k * HD).astype(jnp.bfloat16).astype(jnp.float32)
        for k in range(local_kv)
    ]
    for head in range(heads):
        vector = rotated(2 * key_width + head * HD)
        own = jnp.sum(vector * new_keys[head // group], axis=1, keepdims=True) * score_scale
        flat_query[head * listed : (head + 1) * listed, :] = vector
        flat_own[head * listed : (head + 1) * listed, :] = jnp.broadcast_to(own, (listed, HD))
    lanes = lax.broadcasted_iota(jnp.int32, (heads, HD), 1)
    head_kv = lax.broadcasted_iota(jnp.int32, (heads, HD), 0) // group

    owns, mine = [], []
    for row in range(listed):
        home = row // per_home
        request = listed_at(routes, me, row)
        taken = jnp.int32(0)
        for owner in range(pool_count):
            for place in range(per_home):
                same = routes[owner, place, home] == request
                taken = taken | ((owner < me) & same).astype(jnp.int32)
        vector = flat_query[pl.ds(row, heads, stride=listed), :]
        query[row] = jnp.concatenate(
            [jnp.where(head_kv == k, vector, 0.0) for k in range(local_kv)], axis=1
        ).astype(jnp.bfloat16)
        own = flat_own[pl.ds(row, heads, stride=listed), :]
        own = jnp.where(taken == 0, own, NEG_FILL)
        owns.append(own)
        mine.append(taken == 0)
        peak[row] = own

    def slot_of(slot):
        entry = slot_route[slot]
        row = jnp.maximum(entry, 0)
        length = jnp.where(entry >= 0, context_len[listed_at(routes, me, row)], 0)
        return row, length - slot_block[slot] * BS

    for slot in range(slots):
        row, limit = slot_of(slot)
        value = (
            lax.dot_general(
                query[row],
                keys[slot],
                (((1,), (1,)), ((), ())),
                preferred_element_type=jnp.float32,
            )
            * score_scale
        )
        value = jnp.where(lanes < limit, value, NEG_FILL)
        score[slot] = value
        peak[row] = jnp.maximum(peak[row], value)
    for row in range(listed):
        top = jnp.broadcast_to(jnp.max(peak[row], axis=1, keepdims=True), (heads, HD))
        peak[row] = top
        weight = jnp.where(mine[row], jnp.exp(owns[row] - top), 0.0)
        mass[row] = jnp.where(lanes == 0, weight, 0.0)
        fresh = jnp.zeros((heads, HD), jnp.float32)
        for k in range(local_kv):
            fresh = jnp.where(
                head_kv == k, jnp.broadcast_to(new_values[k][row : row + 1], (heads, HD)), fresh
            )
        total[row] = weight * fresh
    for slot in range(slots):
        row, limit = slot_of(slot)
        expo = jnp.where(lanes < limit, jnp.exp(score[slot] - peak[row]), 0.0)
        mass[row] += expo
        wide = jnp.dot(
            expo.astype(jnp.bfloat16), values[slot], preferred_element_type=jnp.float32
        )
        product = wide[:, :HD]
        for k in range(1, local_kv):
            product = jnp.where(head_kv == k, wide[:, k * HD : (k + 1) * HD], product)
        total[row] += product
    stats = jnp.zeros((heads, HD), jnp.float32)
    for row in range(listed):
        row_mass = jnp.sum(mass[row], axis=1, keepdims=True)
        row_peak = peak[row]
        out[row] = jnp.where(
            row_mass > 0.0, total[row] / jnp.where(row_mass > 0.0, row_mass, 1.0), 0.0
        ).astype(jnp.bfloat16)
        for first, left in ((0, row_peak), (3, row_mass)):
            for piece in range(first, first + 3):
                part = left.astype(jnp.bfloat16).astype(jnp.float32)
                stats = jnp.where(lanes == piece * listed + row, part, stats)
                left = left - part
    out[listed] = stats.astype(jnp.bfloat16)


def merge_kernel(pool_count, routes, *rest):
    parts, (w_out, out) = rest[:pool_count], rest[pool_count : pool_count + 2]
    best, numerator, denominator, flat = rest[pool_count + 2 :]
    listed = parts[0].shape[0] - 1
    requests, heads = best.shape[:2]
    me = lax.axis_index("pool")
    best[...] = jnp.full(best.shape, NEG_FILL, jnp.float32)
    numerator[...] = jnp.zeros_like(numerator)
    denominator[...] = jnp.zeros_like(denominator)
    entries = []
    for shift in range(pool_count):
        owner = lax.rem(me + pool_count - shift, pool_count)
        stats = parts[shift][listed].astype(jnp.float32)
        for row in range(listed):
            request = listed_at(routes, owner, row)
            pieces = [
                stats[:, piece * listed + row : piece * listed + row + 1] for piece in range(6)
            ]
            peak = jnp.broadcast_to(pieces[0] + pieces[1] + pieces[2], (heads, HD))
            mass = jnp.broadcast_to(pieces[3] + pieces[4] + pieces[5], (heads, HD))
            entries.append((shift, row, request, peak, mass))
            best[request] = jnp.maximum(best[request], peak)
    for shift, row, request, peak, mass in entries:
        weight = jnp.exp(peak - best[request]) * mass
        numerator[request] += weight * parts[shift][row].astype(jnp.float32)
        denominator[request] += weight
    for request in range(requests):
        flat[request * heads : (request + 1) * heads, :] = (
            numerator[request] / denominator[request]
        )
    attention = jnp.concatenate(
        [flat[pl.ds(head, requests, stride=heads), :].astype(jnp.bfloat16) for head in range(heads)],
        axis=1,
    )
    for first in range(0, out.shape[1], CHUNK):
        out[:, first : first + CHUNK] = jnp.dot(
            attention, w_out[:, first : first + CHUNK], preferred_element_type=jnp.float32
        )


def shifted(value, axis, shift):
    count = lax.axis_size(axis)
    return lax.ppermute(value, axis, [(i, (i + shift) % count) for i in range(count)])


def in_hbm(value):
    return pltpu.with_memory_space_constraint(value, pltpu.HBM)


def pin(value):
    return pltpu.with_memory_space_constraint(value, pltpu.VMEM)


def close_pool(
    residual,
    norm_gain,
    w_query,
    w_key,
    w_value,
    w_out,
    k_cache,
    v_cache,
    context_len,
    routes,
    slot_route,
    slot_block,
):
    pool_count = lax.axis_size("pool")
    requests, depth = residual.shape
    query_width, key_width = w_query.shape[1], w_key.shape[1]
    heads, local_kv = query_width // HD, key_width // HD
    group = heads // local_kv
    listed = routes.shape[1] * routes.shape[2]
    slots = k_cache.shape[0]
    width = query_width + 2 * key_width
    routes = routes.transpose(0, 2, 1)
    in_smem = pl.BlockSpec(memory_space=pltpu.SMEM)
    in_vmem = pl.BlockSpec(memory_space=pltpu.VMEM)
    in_any = pl.BlockSpec(memory_space=pl.ANY)
    f32 = jnp.float32
    spell = pl.CostEstimate(flops=0, bytes_accessed=2**25, transcendentals=0)

    squares = pl.pallas_call(
        square_kernel,
        out_shape=jax.ShapeDtypeStruct((requests, HD), f32),
        in_specs=[in_vmem],
        out_specs=in_vmem,
        compiler_params=pltpu.CompilerParams(vmem_limit_bytes=4 * 2**20),
        cost_estimate=spell,
        name="square",
    )(residual)
    early = depth * 5 // 8 // CHUNK * CHUNK
    late = (depth - early) // CHUNK
    near_key, near_value, near_query = load(
        squares, (w_key, depth), (w_value, depth), (w_query, early)
    )
    sent = pl.pallas_call(
        functools.partial(project_kernel, pool_count),
        out_shape=[jax.ShapeDtypeStruct((listed, width), f32)] * pool_count,
        in_specs=[in_smem] + [in_vmem] * (pool_count + 5) + [in_any],
        out_specs=[in_vmem] * pool_count,
        scratch_shapes=[
            pltpu.VMEM((late, CHUNK, query_width), jnp.bfloat16),
            pltpu.SemaphoreType.DMA((late,)),
        ],
        compiler_params=pltpu.CompilerParams(vmem_limit_bytes=12 * 2**20),
        cost_estimate=spell,
        name="project",
    )(
        routes,
        residual,
        norm_gain,
        squares,
        *[shifted(squares, "pool", shift) for shift in range(1, pool_count)],
        pin(near_key),
        pin(near_value),
        pin(near_query),
        in_hbm(w_query),
    )
    received = [sent[0]] + [
        shifted((sent[shift] * GROW).astype(jnp.float16), "pool", shift).astype(f32)
        for shift in range(1, pool_count)
    ]
    frequencies = THETA ** (-2.0 * jnp.arange(HD // 2, dtype=f32) / HD)
    late_len, _ = lax.optimization_barrier((context_len, sent[0]))
    angles = late_len.astype(f32)[:, None] * frequencies[None, :]
    cosine, sine = jnp.cos(angles), jnp.sin(angles)
    turn = jnp.concatenate([cosine, cosine, -sine, sine], axis=1)
    near_k, near_v = load(sent[0], (k_cache, slots), (v_cache, slots))
    partial = pl.pallas_call(
        functools.partial(attend_kernel, pool_count, local_kv, group),
        out_shape=jax.ShapeDtypeStruct((listed + 1, heads, HD), jnp.bfloat16),
        in_specs=[in_smem] * 4 + [in_vmem] * (pool_count + 3),
        out_specs=in_vmem,
        scratch_shapes=[
            pltpu.VMEM((listed, 2 * HD), f32),
            pltpu.VMEM((heads * listed, HD), f32),
            pltpu.VMEM((heads * listed, HD), f32),
            pltpu.VMEM((listed, heads, key_width), jnp.bfloat16),
            pltpu.VMEM((slots, heads, HD), f32),
            pltpu.VMEM((listed, heads, HD), f32),
            pltpu.VMEM((listed, heads, HD), f32),
            pltpu.VMEM((listed, heads, HD), f32),
        ],
        compiler_params=pltpu.CompilerParams(vmem_limit_bytes=8 * 2**20),
        cost_estimate=spell,
        name="attend",
    )(routes, context_len, slot_route, slot_block, turn, *received, pin(near_k), pin(near_v))
    partials = [partial] + [shifted(partial, "pool", shift) for shift in range(1, pool_count)]
    near_out = w_out

    product = pl.pallas_call(
        functools.partial(merge_kernel, pool_count),
        out_shape=jax.ShapeDtypeStruct((requests, w_out.shape[1]), f32),
        in_specs=[in_smem] + [in_vmem] * (pool_count + 1),
        out_specs=in_vmem,
        scratch_shapes=[
            pltpu.VMEM((requests, heads, HD), f32),
            pltpu.VMEM((requests, heads, HD), f32),
            pltpu.VMEM((requests, heads, HD), f32),
            pltpu.VMEM((requests * heads, HD), f32),
        ],
        compiler_params=pltpu.CompilerParams(vmem_limit_bytes=8 * 2**20),
        cost_estimate=spell,
        name="merge",
    )(routes, *partials, pin(near_out))
    tensor_count = lax.axis_size("tensor")
    distance = 1
    while distance < tensor_count:
        last_step = 2 * distance == tensor_count
        if last_step:
            product = product.astype(jnp.bfloat16)
        other = lax.ppermute(
            product, "tensor", [(i, i ^ distance) for i in range(tensor_count)]
        )
        product = product.astype(f32) + other.astype(f32)
        distance *= 2
    return (residual.astype(f32) + product).astype(jnp.bfloat16)


def rotate(vectors, positions):
    half_dim = vectors.shape[-1] // 2
    frequencies = THETA ** (-2.0 * jnp.arange(half_dim, dtype=jnp.float32) / vectors.shape[-1])
    angles = positions.astype(jnp.float32)[:, None] * frequencies[None, :]
    cosine = jnp.cos(angles)[:, None, :]
    sine_part = jnp.sin(angles)[:, None, :]
    first_half = vectors[..., :half_dim]
    second_half = vectors[..., half_dim:]
    return jnp.concatenate(
        [
            first_half * cosine - second_half * sine_part,
            second_half * cosine + first_half * sine_part,
        ],
        axis=-1,
    )


def send_back(parts):
    return (
        lax.all_to_all(parts[0], "pool", split_axis=0, concat_axis=0, tiled=True),
        lax.all_to_all(parts[1], "pool", split_axis=0, concat_axis=0, tiled=True),
        lax.all_to_all(parts[2], "pool", split_axis=0, concat_axis=0, tiled=True),
    )


def wide_pool(
    residual,
    norm_gain,
    w_query,
    w_key,
    w_value,
    w_out,
    k_cache,
    v_cache,
    context_len,
    routes,
    slot_route,
    slot_block,
):
    pool_count = lax.axis_size("pool")
    pool_index = lax.axis_index("pool")
    request_count = residual.shape[0]
    per_home = request_count // pool_count
    home_first = pool_index * per_home
    query_width = w_query.shape[1]
    key_width = w_key.shape[1]
    local_heads = query_width // HD
    local_kv = key_width // HD
    group_size = local_heads // local_kv
    slot_count = k_cache.shape[0]
    score_scale = 1.0 / math.sqrt(HD)
    resid_f = residual.astype(jnp.float32)
    square_total = lax.psum(jnp.sum(resid_f * resid_f, axis=1), "pool")
    normed = (
        resid_f
        * lax.rsqrt(square_total / D + EPSILON)[:, None]
        * norm_gain.astype(jnp.float32)[None, :]
    ).astype(jnp.bfloat16)
    owner_routes = lax.dynamic_slice_in_dim(routes, pool_index, 1, 0)[0].reshape(-1)
    slot_request = jnp.where(slot_route >= 0, owner_routes[jnp.maximum(slot_route, 0)], -1)
    key_blocks = k_cache.reshape(slot_count, BS, local_kv, HD)
    value_blocks = v_cache.reshape(slot_count, BS, local_kv, HD)
    positions = slot_block[:, None] * BS + jnp.arange(BS, dtype=jnp.int32)[None, :]
    sent_ids = lax.dynamic_slice_in_dim(routes, pool_index, 1, 1)[:, 0, :]
    home_rows = lax.psum_scatter(
        jnp.concatenate(
            [
                jnp.dot(normed, w_query, preferred_element_type=jnp.float32),
                jnp.dot(normed, w_key, preferred_element_type=jnp.float32),
                jnp.dot(normed, w_value, preferred_element_type=jnp.float32),
            ],
            axis=1,
        ),
        "pool",
        scatter_dimension=0,
        tiled=True,
    )
    home_len = lax.dynamic_slice_in_dim(context_len, home_first, per_home, 0)
    row_total = home_rows.shape[0]
    query = rotate(home_rows[:, :query_width].reshape(row_total, local_heads, HD), home_len).astype(
        jnp.bfloat16
    )
    key_new = rotate(
        home_rows[:, query_width : query_width + key_width].reshape(row_total, local_kv, HD),
        home_len,
    ).astype(jnp.bfloat16)
    value_new = (
        home_rows[:, query_width + key_width :]
        .astype(jnp.bfloat16)
        .reshape(row_total, local_kv, HD)
    )
    home_query = query.reshape(row_total, query_width)
    sent_query = home_query[sent_ids - home_first]
    sent_info = jnp.stack([sent_ids, context_len[sent_ids]], axis=-1)
    rows_query = lax.all_to_all(sent_query, "pool", split_axis=0, concat_axis=0, tiled=True)
    rows_info = lax.all_to_all(sent_info, "pool", split_axis=0, concat_axis=0, tiled=True)
    home_total = rows_query.shape[0]
    item_total = rows_query.shape[1]
    flat_query = rows_query.reshape(home_total * item_total, query_width)
    flat_ids = rows_info[..., 0].reshape(-1)
    flat_len = rows_info[..., 1].reshape(-1)
    matches = slot_request[:, None] == flat_ids[None, :]
    slot_query = jnp.dot(
        matches.astype(jnp.bfloat16), flat_query, preferred_element_type=jnp.float32
    ).astype(jnp.bfloat16)
    grouped = slot_query.reshape(slot_count, local_kv, group_size, HD)
    slot_len = jnp.sum(jnp.where(matches, flat_len[None, :], 0), axis=1)
    present = jnp.any(matches, axis=1)
    in_range = present[:, None] & (positions < slot_len[:, None])
    valid_mask = in_range[:, None, None, :]
    scores = (
        jnp.einsum("skgd,sbkd->skgb", grouped, key_blocks, preferred_element_type=jnp.float32)
        * score_scale
    )
    block_peak = jnp.max(jnp.where(valid_mask, scores, NEG_FILL), axis=3)
    exponent = jnp.exp(jnp.where(valid_mask, scores - block_peak[..., None], NEG_FILL))
    weights = exponent.astype(jnp.bfloat16)
    block_sum = jnp.einsum(
        "skgb,sbkd->skgd", weights, value_blocks, preferred_element_type=jnp.float32
    )
    block_mass = jnp.sum(exponent, axis=3)
    hits = matches.T
    row_peak = jnp.max(jnp.where(hits[:, :, None, None], block_peak[None], NEG_FILL), axis=1)
    factor = jnp.where(hits[:, :, None, None], jnp.exp(block_peak[None] - row_peak[:, None]), 0.0)
    row_sum = jnp.einsum("rskg,skgd->rkgd", factor, block_sum, precision=EXACT)
    row_mass = jnp.einsum("rskg,skg->rkg", factor, block_mass, precision=EXACT)
    back_sum, back_peak, back_mass = send_back(
        (
            row_sum.reshape(home_total, item_total, query_width),
            row_peak.reshape(home_total, item_total, local_heads),
            row_mass.reshape(home_total, item_total, local_heads),
        )
    )
    local_ids = (sent_ids - home_first).reshape(-1)
    owned = local_ids[:, None] == jnp.arange(per_home, dtype=jnp.int32)[None, :]
    sum_rows = back_sum.reshape(-1, local_kv, group_size, HD)
    peak_rows = back_peak.reshape(-1, local_kv, group_size)
    mass_rows = back_mass.reshape(-1, local_kv, group_size)
    query_grid = home_query.reshape(per_home, local_kv, group_size, HD)
    own_score = (
        jnp.einsum("rkgd,rkd->rkg", query_grid, key_new, preferred_element_type=jnp.float32)
        * score_scale
    )
    overall = jnp.maximum(
        own_score, jnp.max(jnp.where(owned[:, :, None, None], peak_rows[:, None], NEG_FILL), axis=0)
    )
    merge_weight = jnp.where(
        owned[:, :, None, None], jnp.exp(peak_rows[:, None] - overall[None]), 0.0
    )
    own_weight = jnp.exp(own_score - overall)
    numerator = (
        jnp.einsum("prkg,pkgd->rkgd", merge_weight, sum_rows, precision=EXACT)
        + own_weight[..., None] * value_new.astype(jnp.float32)[:, :, None, :]
    )
    denominator = jnp.einsum("prkg,pkg->rkg", merge_weight, mass_rows, precision=EXACT) + own_weight
    attention = (
        (numerator / denominator[..., None]).astype(jnp.bfloat16).reshape(per_home, query_width)
    )
    partial_out = jnp.dot(
        lax.all_gather(attention, "pool", axis=0, tiled=True),
        w_out,
        preferred_element_type=jnp.float32,
    )
    head_total = lax.psum(partial_out, "tensor")
    return (resid_f + head_total).astype(jnp.bfloat16)


def solution(mesh):
    placed = (
        P("groups", "pool"),
        P("pool"),
        P("pool", "tensor"),
        P("pool", "tensor"),
        P("pool", "tensor"),
        P("tensor", "pool"),
        P(("groups", "pool"), None, "tensor"),
        P(("groups", "pool"), None, "tensor"),
        P("groups"),
        P("groups", None, None),
        P(("groups", "pool")),
        P(("groups", "pool")),
    )
    pool_count, tensor_count = mesh.shape["pool"], mesh.shape["tensor"]
    close = pool_count <= 4 and tensor_count & (tensor_count - 1) == 0
    return jax.shard_map(
        close_pool if close else wide_pool,
        mesh=mesh,
        in_specs=placed,
        out_specs=P("groups", "pool"),
        check_vma=False,
    )
```

```python
import functools
import math

import jax
import jax.numpy as jnp
from jax import lax
from jax.experimental import pallas as pl
from jax.experimental.pallas import tpu as pltpu
from jax.sharding import PartitionSpec as P

D = 8192
HD = 128
BS = 128

EPSILON = 1e-05
THETA = 500000.0
NEG_FILL = -1e30
EXACT = lax.Precision.HIGHEST
CHUNK = 256
GROW = 128.0


def listed_at(routes, owner, row):
    per_home = routes.shape[1]
    return routes[owner, row % per_home, row // per_home]


def square_kernel(residual, out):
    resid_f = residual[...].astype(jnp.float32)
    out[...] = jnp.broadcast_to(
        jnp.sum(resid_f * resid_f, axis=1, keepdims=True), out.shape
    )


def project_kernel(pool_count, routes, residual, gain, *rest):
    squares, rest = rest[:pool_count], rest[pool_count:]
    weights, outs = rest[:3], rest[3:]
    listed = outs[0].shape[0]
    requests = residual.shape[0]
    rows = pool_count * listed
    me = lax.axis_index("pool")
    total = squares[0][...]
    for part in squares[1:]:
        total = total + part[...]
    scale = lax.rsqrt(total[:, :1] / D + EPSILON)
    resid_f = residual[...].astype(jnp.float32)
    normed = resid_f * scale * gain[...].astype(jnp.float32)[None, :]
    row_ids = lax.broadcasted_iota(jnp.int32, (rows, requests), 0)
    column_ids = lax.broadcasted_iota(jnp.int32, (rows, requests), 1)
    wanted = jnp.zeros((rows, requests), jnp.int32)
    for shift in range(pool_count):
        owner = lax.rem(me + shift, pool_count)
        for row in range(listed):
            wanted = jnp.where(
                row_ids == shift * listed + row, listed_at(routes, owner, row), wanted
            )
    pick = (column_ids == wanted).astype(jnp.float32).astype(jnp.bfloat16)
    picked = jnp.dot(
        pick, normed.astype(jnp.bfloat16), preferred_element_type=jnp.float32
    ).astype(jnp.bfloat16)
    place = 0
    for source in weights:
        for first in range(0, source.shape[1], CHUNK):
            product = jnp.dot(
                picked, source[:, first : first + CHUNK], preferred_element_type=jnp.float32
            )
            for shift in range(pool_count):
                outs[shift][:, place : place + CHUNK] = product[
                    shift * listed : (shift + 1) * listed
                ]
            place += CHUNK


def attend_kernel(
    pool_count, local_kv, group, routes, context_len, slot_route, slot_block, turn, *rest
):
    parts, (keys, values, out) = rest[:pool_count], rest[pool_count : pool_count + 3]
    turned, flat_query, flat_own, query, score, peak, mass, total = rest[pool_count + 3 :]
    listed = parts[0].shape[0]
    heads = local_kv * group
    slots = keys.shape[0]
    key_width = local_kv * HD
    homes = pool_count
    per_home = listed // homes
    score_scale = 1.0 / math.sqrt(HD)
    me = lax.axis_index("pool")
    for row in range(listed):
        turned[row : row + 1, :] = turn[pl.ds(listed_at(routes, me, row), 1), :]
    cosine, sine = turned[:, :HD], turned[:, HD:]

    def column(first):
        value = parts[1][:, first : first + HD]
        for part in parts[2:]:
            value = value + part[:, first : first + HD]
        return parts[0][:, first : first + HD] + value * (1.0 / GROW)

    def rotated(first):
        vector = column(first)
        vector = vector * cosine + pltpu.roll(vector, HD // 2, 1) * sine
        return vector.astype(jnp.bfloat16).astype(jnp.float32)

    new_keys = [rotated(k * HD) for k in range(local_kv)]
    new_values = [
        column(key_width + k * HD).astype(jnp.bfloat16).astype(jnp.float32)
        for k in range(local_kv)
    ]
    for head in range(heads):
        vector = rotated(2 * key_width + head * HD)
        own = jnp.sum(vector * new_keys[head // group], axis=1, keepdims=True) * score_scale
        flat_query[head * listed : (head + 1) * listed, :] = vector
        flat_own[head * listed : (head + 1) * listed, :] = jnp.broadcast_to(own, (listed, HD))
    lanes = lax.broadcasted_iota(jnp.int32, (heads, HD), 1)
    head_kv = lax.broadcasted_iota(jnp.int32, (heads, HD), 0) // group

    owns, mine = [], []
    for row in range(listed):
        home = row // per_home
        request = listed_at(routes, me, row)
        taken = jnp.int32(0)
        for owner in range(pool_count):
            for place in range(per_home):
                same = routes[owner, place, home] == request
                taken = taken | ((owner < me) & same).astype(jnp.int32)
        vector = flat_query[pl.ds(row, heads, stride=listed), :]
        query[row] = jnp.concatenate(
            [jnp.where(head_kv == k, vector, 0.0) for k in range(local_kv)], axis=1
        ).astype(jnp.bfloat16)
        own = flat_own[pl.ds(row, heads, stride=listed), :]
        own = jnp.where(taken == 0, own, NEG_FILL)
        owns.append(own)
        mine.append(taken == 0)
        peak[row] = own

    def slot_of(slot):
        entry = slot_route[slot]
        row = jnp.maximum(entry, 0)
        length = jnp.where(entry >= 0, context_len[listed_at(routes, me, row)], 0)
        return row, length - slot_block[slot] * BS

    for slot in range(slots):
        row, limit = slot_of(slot)
        value = (
            lax.dot_general(
                query[row],
                keys[slot],
                (((1,), (1,)), ((), ())),
                preferred_element_type=jnp.float32,
            )
            * score_scale
        )
        value = jnp.where(lanes < limit, value, NEG_FILL)
        score[slot] = value
        peak[row] = jnp.maximum(peak[row], value)
    for row in range(listed):
        top = jnp.broadcast_to(jnp.max(peak[row], axis=1, keepdims=True), (heads, HD))
        peak[row] = top
        weight = jnp.where(mine[row], jnp.exp(owns[row] - top), 0.0)
        mass[row] = jnp.where(lanes == 0, weight, 0.0)
        fresh = jnp.zeros((heads, HD), jnp.float32)
        for k in range(local_kv):
            fresh = jnp.where(
                head_kv == k, jnp.broadcast_to(new_values[k][row : row + 1], (heads, HD)), fresh
            )
        total[row] = weight * fresh
    for slot in range(slots):
        row, limit = slot_of(slot)
        expo = jnp.where(lanes < limit, jnp.exp(score[slot] - peak[row]), 0.0)
        mass[row] += expo
        wide = jnp.dot(
            expo.astype(jnp.bfloat16), values[slot], preferred_element_type=jnp.float32
        )
        product = wide[:, :HD]
        for k in range(1, local_kv):
            product = jnp.where(head_kv == k, wide[:, k * HD : (k + 1) * HD], product)
        total[row] += product
    stats = jnp.zeros((heads, HD), jnp.float32)
    for row in range(listed):
        row_mass = jnp.sum(mass[row], axis=1, keepdims=True)
        row_peak = peak[row]
        out[row] = jnp.where(
            row_mass > 0.0, total[row] / jnp.where(row_mass > 0.0, row_mass, 1.0), 0.0
        ).astype(jnp.bfloat16)
        for first, left in ((0, row_peak), (3, row_mass)):
            for piece in range(first, first + 3):
                part = left.astype(jnp.bfloat16).astype(jnp.float32)
                stats = jnp.where(lanes == piece * listed + row, part, stats)
                left = left - part
    out[listed] = stats.astype(jnp.bfloat16)


def merge_kernel(pool_count, routes, *rest):
    parts, (w_out, out) = rest[:pool_count], rest[pool_count : pool_count + 2]
    best, numerator, denominator, flat = rest[pool_count + 2 :]
    listed = parts[0].shape[0] - 1
    requests, heads = best.shape[:2]
    me = lax.axis_index("pool")
    best[...] = jnp.full(best.shape, NEG_FILL, jnp.float32)
    numerator[...] = jnp.zeros_like(numerator)
    denominator[...] = jnp.zeros_like(denominator)
    entries = []
    for place, shift in enumerate([0, *shifts(pool_count)]):
        owner = lax.rem(me + pool_count - shift, pool_count)
        stats = parts[place][listed].astype(jnp.float32)
        for row in range(listed):
            request = listed_at(routes, owner, row)
            pieces = [
                stats[:, piece * listed + row : piece * listed + row + 1] for piece in range(6)
            ]
            peak = jnp.broadcast_to(pieces[0] + pieces[1] + pieces[2], (heads, HD))
            mass = jnp.broadcast_to(pieces[3] + pieces[4] + pieces[5], (heads, HD))
            entries.append((place, row, request, peak, mass))
            best[request] = jnp.maximum(best[request], peak)
    for place, row, request, peak, mass in entries:
        weight = jnp.exp(peak - best[request]) * mass
        numerator[request] += weight * parts[place][row].astype(jnp.float32)
        denominator[request] += weight
    for request in range(requests):
        flat[request * heads : (request + 1) * heads, :] = (
            numerator[request] / denominator[request]
        )
    attention = jnp.concatenate(
        [flat[pl.ds(head, requests, stride=heads), :].astype(jnp.bfloat16) for head in range(heads)],
        axis=1,
    )
    for first in range(0, out.shape[1], CHUNK):
        out[:, first : first + CHUNK] = jnp.dot(
            attention, w_out[:, first : first + CHUNK], preferred_element_type=jnp.float32
        )


def shifts(pool_count):
    return range(pool_count - 1, 0, -1)


def shifted(value, axis, shift):
    count = lax.axis_size(axis)
    return lax.ppermute(value, axis, [(i, (i + shift) % count) for i in range(count)])


def pin(value):
    return pltpu.with_memory_space_constraint(value, pltpu.VMEM)


def close_pool(
    residual,
    norm_gain,
    w_query,
    w_key,
    w_value,
    w_out,
    k_cache,
    v_cache,
    context_len,
    routes,
    slot_route,
    slot_block,
):
    pool_count = lax.axis_size("pool")
    requests, depth = residual.shape
    query_width, key_width = w_query.shape[1], w_key.shape[1]
    heads, local_kv = query_width // HD, key_width // HD
    group = heads // local_kv
    listed = routes.shape[1] * routes.shape[2]
    slots = k_cache.shape[0]
    width = query_width + 2 * key_width
    routes = routes.transpose(0, 2, 1)
    in_smem = pl.BlockSpec(memory_space=pltpu.SMEM)
    in_vmem = pl.BlockSpec(memory_space=pltpu.VMEM)
    f32 = jnp.float32
    spell = pl.CostEstimate(flops=2**34, bytes_accessed=2**25, transcendentals=0)

    squares = pl.pallas_call(
        square_kernel,
        out_shape=jax.ShapeDtypeStruct((requests, HD), f32),
        in_specs=[in_vmem],
        out_specs=in_vmem,
        compiler_params=pltpu.CompilerParams(vmem_limit_bytes=4 * 2**20),
        cost_estimate=spell,
        name="square",
    )(residual)
    sent = pl.pallas_call(
        functools.partial(project_kernel, pool_count),
        out_shape=[jax.ShapeDtypeStruct((listed, width), f32)] * pool_count,
        in_specs=[in_smem] + [in_vmem] * (pool_count + 5),
        out_specs=[in_vmem] * pool_count,
        compiler_params=pltpu.CompilerParams(vmem_limit_bytes=8 * 2**20),
        cost_estimate=spell,
        name="project",
    )(
        routes,
        residual,
        norm_gain,
        squares,
        *[shifted(squares, "pool", shift) for shift in shifts(pool_count)],
        pin(w_key),
        pin(w_value),
        pin(w_query),
    )
    received = [sent[0]] + [
        shifted((sent[shift] * GROW).astype(jnp.float16), "pool", shift).astype(f32)
        for shift in shifts(pool_count)
    ]
    frequencies = THETA ** (-2.0 * jnp.arange(HD // 2, dtype=f32) / HD)
    late_len, _ = lax.optimization_barrier((context_len, sent[0]))
    angles = late_len.astype(f32)[:, None] * frequencies[None, :]
    cosine, sine = jnp.cos(angles), jnp.sin(angles)
    turn = jnp.concatenate([cosine, cosine, -sine, sine], axis=1)
    partial = pl.pallas_call(
        functools.partial(attend_kernel, pool_count, local_kv, group),
        out_shape=jax.ShapeDtypeStruct((listed + 1, heads, HD), jnp.bfloat16),
        in_specs=[in_smem] * 4 + [in_vmem] * (pool_count + 3),
        out_specs=in_vmem,
        scratch_shapes=[
            pltpu.VMEM((listed, 2 * HD), f32),
            pltpu.VMEM((heads * listed, HD), f32),
            pltpu.VMEM((heads * listed, HD), f32),
            pltpu.VMEM((listed, heads, key_width), jnp.bfloat16),
            pltpu.VMEM((slots, heads, HD), f32),
            pltpu.VMEM((listed, heads, HD), f32),
            pltpu.VMEM((listed, heads, HD), f32),
            pltpu.VMEM((listed, heads, HD), f32),
        ],
        compiler_params=pltpu.CompilerParams(vmem_limit_bytes=8 * 2**20),
        cost_estimate=spell,
        name="attend",
    )(routes, context_len, slot_route, slot_block, turn, *received, pin(k_cache), pin(v_cache))
    partials = [partial] + [shifted(partial, "pool", shift) for shift in shifts(pool_count)]

    product = pl.pallas_call(
        functools.partial(merge_kernel, pool_count),
        out_shape=jax.ShapeDtypeStruct((requests, w_out.shape[1]), f32),
        in_specs=[in_smem] + [in_vmem] * (pool_count + 1),
        out_specs=in_vmem,
        scratch_shapes=[
            pltpu.VMEM((requests, heads, HD), f32),
            pltpu.VMEM((requests, heads, HD), f32),
            pltpu.VMEM((requests, heads, HD), f32),
            pltpu.VMEM((requests * heads, HD), f32),
        ],
        compiler_params=pltpu.CompilerParams(vmem_limit_bytes=8 * 2**20),
        cost_estimate=spell,
        name="merge",
    )(routes, *partials, pin(w_out))
    tensor_count = lax.axis_size("tensor")
    distance = 1
    while distance < tensor_count:
        last_step = 2 * distance == tensor_count
        if last_step:
            product = product.astype(jnp.bfloat16)
        other = lax.ppermute(
            product, "tensor", [(i, i ^ distance) for i in range(tensor_count)]
        )
        product = product.astype(f32) + other.astype(f32)
        distance *= 2
    return (residual.astype(f32) + product).astype(jnp.bfloat16)


def rotate(vectors, positions):
    half_dim = vectors.shape[-1] // 2
    frequencies = THETA ** (-2.0 * jnp.arange(half_dim, dtype=jnp.float32) / vectors.shape[-1])
    angles = positions.astype(jnp.float32)[:, None] * frequencies[None, :]
    cosine = jnp.cos(angles)[:, None, :]
    sine_part = jnp.sin(angles)[:, None, :]
    first_half = vectors[..., :half_dim]
    second_half = vectors[..., half_dim:]
    return jnp.concatenate(
        [
            first_half * cosine - second_half * sine_part,
            second_half * cosine + first_half * sine_part,
        ],
        axis=-1,
    )


def send_back(parts):
    return (
        lax.all_to_all(parts[0], "pool", split_axis=0, concat_axis=0, tiled=True),
        lax.all_to_all(parts[1], "pool", split_axis=0, concat_axis=0, tiled=True),
        lax.all_to_all(parts[2], "pool", split_axis=0, concat_axis=0, tiled=True),
    )


def wide_pool(
    residual,
    norm_gain,
    w_query,
    w_key,
    w_value,
    w_out,
    k_cache,
    v_cache,
    context_len,
    routes,
    slot_route,
    slot_block,
):
    pool_count = lax.axis_size("pool")
    pool_index = lax.axis_index("pool")
    request_count = residual.shape[0]
    per_home = request_count // pool_count
    home_first = pool_index * per_home
    query_width = w_query.shape[1]
    key_width = w_key.shape[1]
    local_heads = query_width // HD
    local_kv = key_width // HD
    group_size = local_heads // local_kv
    slot_count = k_cache.shape[0]
    score_scale = 1.0 / math.sqrt(HD)
    resid_f = residual.astype(jnp.float32)
    square_total = lax.psum(jnp.sum(resid_f * resid_f, axis=1), "pool")
    normed = (
        resid_f
        * lax.rsqrt(square_total / D + EPSILON)[:, None]
        * norm_gain.astype(jnp.float32)[None, :]
    ).astype(jnp.bfloat16)
    owner_routes = lax.dynamic_slice_in_dim(routes, pool_index, 1, 0)[0].reshape(-1)
    slot_request = jnp.where(slot_route >= 0, owner_routes[jnp.maximum(slot_route, 0)], -1)
    key_blocks = k_cache.reshape(slot_count, BS, local_kv, HD)
    value_blocks = v_cache.reshape(slot_count, BS, local_kv, HD)
    positions = slot_block[:, None] * BS + jnp.arange(BS, dtype=jnp.int32)[None, :]
    sent_ids = lax.dynamic_slice_in_dim(routes, pool_index, 1, 1)[:, 0, :]
    home_rows = lax.psum_scatter(
        jnp.concatenate(
            [
                jnp.dot(normed, w_query, preferred_element_type=jnp.float32),
                jnp.dot(normed, w_key, preferred_element_type=jnp.float32),
                jnp.dot(normed, w_value, preferred_element_type=jnp.float32),
            ],
            axis=1,
        ),
        "pool",
        scatter_dimension=0,
        tiled=True,
    )
    home_len = lax.dynamic_slice_in_dim(context_len, home_first, per_home, 0)
    row_total = home_rows.shape[0]
    query = rotate(home_rows[:, :query_width].reshape(row_total, local_heads, HD), home_len).astype(
        jnp.bfloat16
    )
    key_new = rotate(
        home_rows[:, query_width : query_width + key_width].reshape(row_total, local_kv, HD),
        home_len,
    ).astype(jnp.bfloat16)
    value_new = (
        home_rows[:, query_width + key_width :]
        .astype(jnp.bfloat16)
        .reshape(row_total, local_kv, HD)
    )
    home_query = query.reshape(row_total, query_width)
    sent_query = home_query[sent_ids - home_first]
    sent_info = jnp.stack([sent_ids, context_len[sent_ids]], axis=-1)
    rows_query = lax.all_to_all(sent_query, "pool", split_axis=0, concat_axis=0, tiled=True)
    rows_info = lax.all_to_all(sent_info, "pool", split_axis=0, concat_axis=0, tiled=True)
    home_total = rows_query.shape[0]
    item_total = rows_query.shape[1]
    flat_query = rows_query.reshape(home_total * item_total, query_width)
    flat_ids = rows_info[..., 0].reshape(-1)
    flat_len = rows_info[..., 1].reshape(-1)
    matches = slot_request[:, None] == flat_ids[None, :]
    slot_query = jnp.dot(
        matches.astype(jnp.bfloat16), flat_query, preferred_element_type=jnp.float32
    ).astype(jnp.bfloat16)
    grouped = slot_query.reshape(slot_count, local_kv, group_size, HD)
    slot_len = jnp.sum(jnp.where(matches, flat_len[None, :], 0), axis=1)
    present = jnp.any(matches, axis=1)
    in_range = present[:, None] & (positions < slot_len[:, None])
    valid_mask = in_range[:, None, None, :]
    scores = (
        jnp.einsum("skgd,sbkd->skgb", grouped, key_blocks, preferred_element_type=jnp.float32)
        * score_scale
    )
    block_peak = jnp.max(jnp.where(valid_mask, scores, NEG_FILL), axis=3)
    exponent = jnp.exp(jnp.where(valid_mask, scores - block_peak[..., None], NEG_FILL))
    weights = exponent.astype(jnp.bfloat16)
    block_sum = jnp.einsum(
        "skgb,sbkd->skgd", weights, value_blocks, preferred_element_type=jnp.float32
    )
    block_mass = jnp.sum(exponent, axis=3)
    hits = matches.T
    row_peak = jnp.max(jnp.where(hits[:, :, None, None], block_peak[None], NEG_FILL), axis=1)
    factor = jnp.where(hits[:, :, None, None], jnp.exp(block_peak[None] - row_peak[:, None]), 0.0)
    row_sum = jnp.einsum("rskg,skgd->rkgd", factor, block_sum, precision=EXACT)
    row_mass = jnp.einsum("rskg,skg->rkg", factor, block_mass, precision=EXACT)
    back_sum, back_peak, back_mass = send_back(
        (
            row_sum.reshape(home_total, item_total, query_width),
            row_peak.reshape(home_total, item_total, local_heads),
            row_mass.reshape(home_total, item_total, local_heads),
        )
    )
    local_ids = (sent_ids - home_first).reshape(-1)
    owned = local_ids[:, None] == jnp.arange(per_home, dtype=jnp.int32)[None, :]
    sum_rows = back_sum.reshape(-1, local_kv, group_size, HD)
    peak_rows = back_peak.reshape(-1, local_kv, group_size)
    mass_rows = back_mass.reshape(-1, local_kv, group_size)
    query_grid = home_query.reshape(per_home, local_kv, group_size, HD)
    own_score = (
        jnp.einsum("rkgd,rkd->rkg", query_grid, key_new, preferred_element_type=jnp.float32)
        * score_scale
    )
    overall = jnp.maximum(
        own_score, jnp.max(jnp.where(owned[:, :, None, None], peak_rows[:, None], NEG_FILL), axis=0)
    )
    merge_weight = jnp.where(
        owned[:, :, None, None], jnp.exp(peak_rows[:, None] - overall[None]), 0.0
    )
    own_weight = jnp.exp(own_score - overall)
    numerator = (
        jnp.einsum("prkg,pkgd->rkgd", merge_weight, sum_rows, precision=EXACT)
        + own_weight[..., None] * value_new.astype(jnp.float32)[:, :, None, :]
    )
    denominator = jnp.einsum("prkg,pkg->rkg", merge_weight, mass_rows, precision=EXACT) + own_weight
    attention = (
        (numerator / denominator[..., None]).astype(jnp.bfloat16).reshape(per_home, query_width)
    )
    partial_out = jnp.dot(
        lax.all_gather(attention, "pool", axis=0, tiled=True),
        w_out,
        preferred_element_type=jnp.float32,
    )
    head_total = lax.psum(partial_out, "tensor")
    return (resid_f + head_total).astype(jnp.bfloat16)


def solution(mesh):
    placed = (
        P("groups", "pool"),
        P("pool"),
        P("pool", "tensor"),
        P("pool", "tensor"),
        P("pool", "tensor"),
        P("tensor", "pool"),
        P(("groups", "pool"), None, "tensor"),
        P(("groups", "pool"), None, "tensor"),
        P("groups"),
        P("groups", None, None),
        P(("groups", "pool")),
        P(("groups", "pool")),
    )
    pool_count, tensor_count = mesh.shape["pool"], mesh.shape["tensor"]
    close = pool_count <= 4 and tensor_count & (tensor_count - 1) == 0
    return jax.shard_map(
        close_pool if close else wide_pool,
        mesh=mesh,
        in_specs=placed,
        out_specs=P("groups", "pool"),
        check_vma=False,
    )
```

```python
import functools
import math

import jax
import jax.numpy as jnp
from jax import lax
from jax.experimental import pallas as pl
from jax.experimental.pallas import tpu as pltpu
from jax.sharding import PartitionSpec as P

D = 8192
HD = 128
BS = 128

EPSILON = 1e-05
THETA = 500000.0
NEG_FILL = -1e30
EXACT = lax.Precision.HIGHEST
CHUNK = 256
GROW = 128.0


def listed_at(routes, owner, row):
    per_home = routes.shape[1]
    return routes[owner, row % per_home, row // per_home]


def square_kernel(residual, out):
    resid_f = residual[...].astype(jnp.float32)
    out[...] = jnp.broadcast_to(
        jnp.sum(resid_f * resid_f, axis=1, keepdims=True), out.shape
    )


def project_kernel(pool_count, routes, residual, gain, *rest):
    squares, rest = rest[:pool_count], rest[pool_count:]
    weights, outs = rest[:3], rest[3:]
    listed = outs[0].shape[0]
    requests = residual.shape[0]
    rows = pool_count * listed
    me = lax.axis_index("pool")
    total = squares[0][...]
    for part in squares[1:]:
        total = total + part[...]
    scale = lax.rsqrt(total[:, :1] / D + EPSILON)
    resid_f = residual[...].astype(jnp.float32)
    normed = resid_f * scale * gain[...].astype(jnp.float32)[None, :]
    row_ids = lax.broadcasted_iota(jnp.int32, (rows, requests), 0)
    column_ids = lax.broadcasted_iota(jnp.int32, (rows, requests), 1)
    wanted = jnp.zeros((rows, requests), jnp.int32)
    for shift in range(pool_count):
        owner = lax.rem(me + shift, pool_count)
        for row in range(listed):
            wanted = jnp.where(
                row_ids == shift * listed + row, listed_at(routes, owner, row), wanted
            )
    pick = (column_ids == wanted).astype(jnp.float32).astype(jnp.bfloat16)
    picked = jnp.dot(
        pick, normed.astype(jnp.bfloat16), preferred_element_type=jnp.float32
    ).astype(jnp.bfloat16)
    place = 0
    for source in weights:
        for first in range(0, source.shape[1], CHUNK):
            product = jnp.dot(
                picked, source[:, first : first + CHUNK], preferred_element_type=jnp.float32
            )
            for shift in range(pool_count):
                outs[shift][:, place : place + CHUNK] = product[
                    shift * listed : (shift + 1) * listed
                ]
            place += CHUNK


def attend_kernel(
    pool_count, local_kv, group, routes, context_len, slot_route, slot_block, turn, *rest
):
    parts, (keys, values, out) = rest[:pool_count], rest[pool_count : pool_count + 3]
    turned, flat_query, flat_own, query, score, peak, mass, total = rest[pool_count + 3 :]
    listed = parts[0].shape[0]
    heads = local_kv * group
    slots = keys.shape[0]
    key_width = local_kv * HD
    homes = pool_count
    per_home = listed // homes
    score_scale = 1.0 / math.sqrt(HD)
    me = lax.axis_index("pool")
    for row in range(listed):
        turned[row : row + 1, :] = turn[pl.ds(listed_at(routes, me, row), 1), :]
    cosine, sine = turned[:, :HD], turned[:, HD:]

    def column(first):
        value = parts[1][:, first : first + HD]
        for part in parts[2:]:
            value = value + part[:, first : first + HD]
        return parts[0][:, first : first + HD] + value * (1.0 / GROW)

    def rotated(first):
        vector = column(first)
        vector = vector * cosine + pltpu.roll(vector, HD // 2, 1) * sine
        return vector.astype(jnp.bfloat16).astype(jnp.float32)

    new_keys = [rotated(k * HD) for k in range(local_kv)]
    new_values = [
        column(key_width + k * HD).astype(jnp.bfloat16).astype(jnp.float32)
        for k in range(local_kv)
    ]
    for head in range(heads):
        vector = rotated(2 * key_width + head * HD)
        own = jnp.sum(vector * new_keys[head // group], axis=1, keepdims=True) * score_scale
        flat_query[head * listed : (head + 1) * listed, :] = vector
        flat_own[head * listed : (head + 1) * listed, :] = jnp.broadcast_to(own, (listed, HD))
    lanes = lax.broadcasted_iota(jnp.int32, (heads, HD), 1)
    head_kv = lax.broadcasted_iota(jnp.int32, (heads, HD), 0) // group

    owns, mine = [], []
    peak[...] = jnp.full(peak.shape, NEG_FILL, jnp.float32)
    for row in range(listed):
        home = row // per_home
        request = listed_at(routes, me, row)
        taken = jnp.int32(0)
        for owner in range(pool_count):
            for place in range(per_home):
                same = routes[owner, place, home] == request
                taken = taken | ((owner < me) & same).astype(jnp.int32)
        vector = flat_query[pl.ds(row, heads, stride=listed), :]
        query[row] = jnp.concatenate(
            [jnp.where(head_kv == k, vector, 0.0) for k in range(local_kv)], axis=1
        ).astype(jnp.bfloat16)
        own = flat_own[pl.ds(row, heads, stride=listed), :]
        own = jnp.where(taken == 0, own, NEG_FILL)
        owns.append(own)
        mine.append(taken == 0)

    def slot_of(slot):
        entry = slot_route[slot]
        row = jnp.maximum(entry, 0)
        length = jnp.where(entry >= 0, context_len[listed_at(routes, me, row)], 0)
        return row, length - slot_block[slot] * BS

    for slot in range(slots):
        row, limit = slot_of(slot)
        value = (
            lax.dot_general(
                query[row],
                keys[slot],
                (((1,), (1,)), ((), ())),
                preferred_element_type=jnp.float32,
            )
            * score_scale
        )
        value = jnp.where(lanes < limit, value, NEG_FILL)
        score[slot] = value
        peak[row] = jnp.maximum(peak[row], value)
    for row in range(listed):
        top = jnp.maximum(jnp.max(peak[row], axis=1, keepdims=True), owns[row])
        peak[row] = top
        weight = jnp.where(mine[row], jnp.exp(owns[row] - top), 0.0)
        mass[row] = jnp.where(lanes == 0, weight, 0.0)
        fresh = jnp.zeros((heads, HD), jnp.float32)
        for k in range(local_kv):
            fresh = jnp.where(
                head_kv == k, jnp.broadcast_to(new_values[k][row : row + 1], (heads, HD)), fresh
            )
        total[row] = weight * fresh
    for slot in range(slots):
        row, limit = slot_of(slot)
        expo = jnp.where(lanes < limit, jnp.exp(score[slot] - peak[row]), 0.0)
        mass[row] += expo
        wide = jnp.dot(
            expo.astype(jnp.bfloat16), values[slot], preferred_element_type=jnp.float32
        )
        product = wide[:, :HD]
        for k in range(1, local_kv):
            product = jnp.where(head_kv == k, wide[:, k * HD : (k + 1) * HD], product)
        total[row] += product
    stats = jnp.zeros((heads, HD), jnp.float32)
    for row in range(listed):
        row_mass = jnp.sum(mass[row], axis=1, keepdims=True)
        row_peak = peak[row]
        out[row] = jnp.where(
            row_mass > 0.0, total[row] / jnp.where(row_mass > 0.0, row_mass, 1.0), 0.0
        ).astype(jnp.bfloat16)
        for first, left in ((0, row_peak), (3, row_mass)):
            for piece in range(first, first + 3):
                part = left.astype(jnp.bfloat16).astype(jnp.float32)
                stats = jnp.where(lanes == piece * listed + row, part, stats)
                left = left - part
    out[listed] = stats.astype(jnp.bfloat16)


def merge_kernel(pool_count, routes, *rest):
    parts, (w_out, out, flat) = rest[:pool_count], rest[pool_count:]
    listed = parts[0].shape[0] - 1
    heads = parts[0].shape[1]
    requests = out.shape[0]
    me = lax.axis_index("pool")
    flat[...] = jnp.zeros_like(flat)
    lanes = lax.broadcasted_iota(jnp.int32, (heads, HD), 1)
    asked, there, peaks, masses = [], [], [], []
    for place, shift in enumerate([0, *shifts(pool_count)]):
        owner = lax.rem(me + pool_count - shift, pool_count)
        asked.append([listed_at(routes, owner, row) for row in range(listed)])
        stats = parts[place][listed].astype(jnp.float32)
        stats = (
            stats + pltpu.roll(stats, HD - listed, 1) + pltpu.roll(stats, HD - 2 * listed, 1)
        )
        source = jnp.full((heads, HD), -1, jnp.int32)
        for row, request in enumerate(asked[-1]):
            source = jnp.where(lanes == request, row, source)
        there.append(source >= 0)
        source = jnp.maximum(source, 0)
        peaks.append(
            jnp.where(there[-1], jnp.take_along_axis(stats, source, axis=1), NEG_FILL)
        )
        masses.append(jnp.take_along_axis(stats, source + 3 * listed, axis=1))
    best = functools.reduce(jnp.maximum, peaks)
    weights = [
        jnp.where(here, jnp.exp(peak - best) * mass, 0.0)
        for here, peak, mass in zip(there, peaks, masses)
    ]
    whole = sum(weights[1:], weights[0])
    whole = jnp.where(lanes < requests, whole, 1.0)
    for place, ids in enumerate(asked):
        back = jnp.zeros((heads, HD), jnp.int32)
        for row, request in enumerate(ids):
            back = jnp.where(lanes == row, request, back)
        weight = jnp.take_along_axis(weights[place] / whole, back, axis=1)
        for row, request in enumerate(ids):
            block = pl.ds(pl.multiple_of(request * heads, heads), heads)
            flat[place, block, :] = weight[:, row : row + 1] * parts[place][row].astype(
                jnp.float32
            )
    columns = []
    for head in range(heads):
        block = pl.ds(head, requests, stride=heads)
        value = flat[0, block, :]
        for place in range(1, pool_count):
            value = value + flat[place, block, :]
        columns.append(value.astype(jnp.bfloat16))
    attention = jnp.concatenate(columns, axis=1)
    for first in range(0, out.shape[1], CHUNK):
        out[:, first : first + CHUNK] = jnp.dot(
            attention, w_out[:, first : first + CHUNK], preferred_element_type=jnp.float32
        )


def shifts(pool_count):
    return range(pool_count - 1, 0, -1)


def shifted(value, axis, shift):
    count = lax.axis_size(axis)
    return lax.ppermute(value, axis, [(i, (i + shift) % count) for i in range(count)])


def pin(value):
    return pltpu.with_memory_space_constraint(value, pltpu.VMEM)


def close_pool(
    residual,
    norm_gain,
    w_query,
    w_key,
    w_value,
    w_out,
    k_cache,
    v_cache,
    context_len,
    routes,
    slot_route,
    slot_block,
):
    pool_count = lax.axis_size("pool")
    requests, depth = residual.shape
    query_width, key_width = w_query.shape[1], w_key.shape[1]
    heads, local_kv = query_width // HD, key_width // HD
    group = heads // local_kv
    listed = routes.shape[1] * routes.shape[2]
    slots = k_cache.shape[0]
    width = query_width + 2 * key_width
    routes = routes.transpose(0, 2, 1)
    in_smem = pl.BlockSpec(memory_space=pltpu.SMEM)
    in_vmem = pl.BlockSpec(memory_space=pltpu.VMEM)
    f32 = jnp.float32
    spell = pl.CostEstimate(flops=2**34, bytes_accessed=2**25, transcendentals=0)

    squares = pl.pallas_call(
        square_kernel,
        out_shape=jax.ShapeDtypeStruct((requests, HD), f32),
        in_specs=[in_vmem],
        out_specs=in_vmem,
        compiler_params=pltpu.CompilerParams(vmem_limit_bytes=4 * 2**20),
        cost_estimate=spell,
        name="square",
    )(residual)
    sent = pl.pallas_call(
        functools.partial(project_kernel, pool_count),
        out_shape=[jax.ShapeDtypeStruct((listed, width), f32)] * pool_count,
        in_specs=[in_smem] + [in_vmem] * (pool_count + 5),
        out_specs=[in_vmem] * pool_count,
        compiler_params=pltpu.CompilerParams(vmem_limit_bytes=8 * 2**20),
        cost_estimate=spell,
        name="project",
    )(
        routes,
        residual,
        norm_gain,
        squares,
        *[shifted(squares, "pool", shift) for shift in shifts(pool_count)],
        pin(w_key),
        pin(w_value),
        pin(w_query),
    )
    received = [sent[0]] + [
        shifted((sent[shift] * GROW).astype(jnp.float16), "pool", shift).astype(f32)
        for shift in shifts(pool_count)
    ]
    frequencies = THETA ** (-2.0 * jnp.arange(HD // 2, dtype=f32) / HD)
    late_len, _ = lax.optimization_barrier((context_len, sent[0]))
    angles = late_len.astype(f32)[:, None] * frequencies[None, :]
    cosine, sine = jnp.cos(angles), jnp.sin(angles)
    turn = jnp.concatenate([cosine, cosine, -sine, sine], axis=1)
    partial = pl.pallas_call(
        functools.partial(attend_kernel, pool_count, local_kv, group),
        out_shape=jax.ShapeDtypeStruct((listed + 1, heads, HD), jnp.bfloat16),
        in_specs=[in_smem] * 4 + [in_vmem] * (pool_count + 3),
        out_specs=in_vmem,
        scratch_shapes=[
            pltpu.VMEM((listed, 2 * HD), f32),
            pltpu.VMEM((heads * listed, HD), f32),
            pltpu.VMEM((heads * listed, HD), f32),
            pltpu.VMEM((listed, heads, key_width), jnp.bfloat16),
            pltpu.VMEM((slots, heads, HD), f32),
            pltpu.VMEM((listed, heads, HD), f32),
            pltpu.VMEM((listed, heads, HD), f32),
            pltpu.VMEM((listed, heads, HD), f32),
        ],
        compiler_params=pltpu.CompilerParams(vmem_limit_bytes=8 * 2**20),
        cost_estimate=spell,
        name="attend",
    )(routes, context_len, slot_route, slot_block, turn, *received, pin(k_cache), pin(v_cache))
    partials = [partial] + [shifted(partial, "pool", shift) for shift in shifts(pool_count)]

    product = pl.pallas_call(
        functools.partial(merge_kernel, pool_count),
        out_shape=jax.ShapeDtypeStruct((requests, w_out.shape[1]), f32),
        in_specs=[in_smem] + [in_vmem] * (pool_count + 1),
        out_specs=in_vmem,
        scratch_shapes=[pltpu.VMEM((pool_count, requests * heads, HD), f32)],
        compiler_params=pltpu.CompilerParams(vmem_limit_bytes=8 * 2**20),
        cost_estimate=spell,
        name="merge",
    )(routes, *partials, pin(w_out))
    tensor_count = lax.axis_size("tensor")
    product = product.astype(jnp.bfloat16)
    one, two, three = [
        lax.ppermute(product, "tensor", [(i, i ^ d) for i in range(tensor_count)]).astype(f32)
        for d in (1, 2, 3)
    ]
    product = product.astype(f32)
    return (residual.astype(f32) + ((product + one) + (two + three))).astype(jnp.bfloat16)


def rotate(vectors, positions):
    half_dim = vectors.shape[-1] // 2
    frequencies = THETA ** (-2.0 * jnp.arange(half_dim, dtype=jnp.float32) / vectors.shape[-1])
    angles = positions.astype(jnp.float32)[:, None] * frequencies[None, :]
    cosine = jnp.cos(angles)[:, None, :]
    sine_part = jnp.sin(angles)[:, None, :]
    first_half = vectors[..., :half_dim]
    second_half = vectors[..., half_dim:]
    return jnp.concatenate(
        [
            first_half * cosine - second_half * sine_part,
            second_half * cosine + first_half * sine_part,
        ],
        axis=-1,
    )


def send_back(parts):
    return (
        lax.all_to_all(parts[0], "pool", split_axis=0, concat_axis=0, tiled=True),
        lax.all_to_all(parts[1], "pool", split_axis=0, concat_axis=0, tiled=True),
        lax.all_to_all(parts[2], "pool", split_axis=0, concat_axis=0, tiled=True),
    )


def wide_pool(
    residual,
    norm_gain,
    w_query,
    w_key,
    w_value,
    w_out,
    k_cache,
    v_cache,
    context_len,
    routes,
    slot_route,
    slot_block,
):
    pool_count = lax.axis_size("pool")
    pool_index = lax.axis_index("pool")
    request_count = residual.shape[0]
    per_home = request_count // pool_count
    home_first = pool_index * per_home
    query_width = w_query.shape[1]
    key_width = w_key.shape[1]
    local_heads = query_width // HD
    local_kv = key_width // HD
    group_size = local_heads // local_kv
    slot_count = k_cache.shape[0]
    score_scale = 1.0 / math.sqrt(HD)
    resid_f = residual.astype(jnp.float32)
    square_total = lax.psum(jnp.sum(resid_f * resid_f, axis=1), "pool")
    normed = (
        resid_f
        * lax.rsqrt(square_total / D + EPSILON)[:, None]
        * norm_gain.astype(jnp.float32)[None, :]
    ).astype(jnp.bfloat16)
    owner_routes = lax.dynamic_slice_in_dim(routes, pool_index, 1, 0)[0].reshape(-1)
    slot_request = jnp.where(slot_route >= 0, owner_routes[jnp.maximum(slot_route, 0)], -1)
    key_blocks = k_cache.reshape(slot_count, BS, local_kv, HD)
    value_blocks = v_cache.reshape(slot_count, BS, local_kv, HD)
    positions = slot_block[:, None] * BS + jnp.arange(BS, dtype=jnp.int32)[None, :]
    sent_ids = lax.dynamic_slice_in_dim(routes, pool_index, 1, 1)[:, 0, :]
    home_rows = lax.psum_scatter(
        jnp.concatenate(
            [
                jnp.dot(normed, w_query, preferred_element_type=jnp.float32),
                jnp.dot(normed, w_key, preferred_element_type=jnp.float32),
                jnp.dot(normed, w_value, preferred_element_type=jnp.float32),
            ],
            axis=1,
        ),
        "pool",
        scatter_dimension=0,
        tiled=True,
    )
    home_len = lax.dynamic_slice_in_dim(context_len, home_first, per_home, 0)
    row_total = home_rows.shape[0]
    query = rotate(home_rows[:, :query_width].reshape(row_total, local_heads, HD), home_len).astype(
        jnp.bfloat16
    )
    key_new = rotate(
        home_rows[:, query_width : query_width + key_width].reshape(row_total, local_kv, HD),
        home_len,
    ).astype(jnp.bfloat16)
    value_new = (
        home_rows[:, query_width + key_width :]
        .astype(jnp.bfloat16)
        .reshape(row_total, local_kv, HD)
    )
    home_query = query.reshape(row_total, query_width)
    sent_query = home_query[sent_ids - home_first]
    sent_info = jnp.stack([sent_ids, context_len[sent_ids]], axis=-1)
    rows_query = lax.all_to_all(sent_query, "pool", split_axis=0, concat_axis=0, tiled=True)
    rows_info = lax.all_to_all(sent_info, "pool", split_axis=0, concat_axis=0, tiled=True)
    home_total = rows_query.shape[0]
    item_total = rows_query.shape[1]
    flat_query = rows_query.reshape(home_total * item_total, query_width)
    flat_ids = rows_info[..., 0].reshape(-1)
    flat_len = rows_info[..., 1].reshape(-1)
    matches = slot_request[:, None] == flat_ids[None, :]
    slot_query = jnp.dot(
        matches.astype(jnp.bfloat16), flat_query, preferred_element_type=jnp.float32
    ).astype(jnp.bfloat16)
    grouped = slot_query.reshape(slot_count, local_kv, group_size, HD)
    slot_len = jnp.sum(jnp.where(matches, flat_len[None, :], 0), axis=1)
    present = jnp.any(matches, axis=1)
    in_range = present[:, None] & (positions < slot_len[:, None])
    valid_mask = in_range[:, None, None, :]
    scores = (
        jnp.einsum("skgd,sbkd->skgb", grouped, key_blocks, preferred_element_type=jnp.float32)
        * score_scale
    )
    block_peak = jnp.max(jnp.where(valid_mask, scores, NEG_FILL), axis=3)
    exponent = jnp.exp(jnp.where(valid_mask, scores - block_peak[..., None], NEG_FILL))
    weights = exponent.astype(jnp.bfloat16)
    block_sum = jnp.einsum(
        "skgb,sbkd->skgd", weights, value_blocks, preferred_element_type=jnp.float32
    )
    block_mass = jnp.sum(exponent, axis=3)
    hits = matches.T
    row_peak = jnp.max(jnp.where(hits[:, :, None, None], block_peak[None], NEG_FILL), axis=1)
    factor = jnp.where(hits[:, :, None, None], jnp.exp(block_peak[None] - row_peak[:, None]), 0.0)
    row_sum = jnp.einsum("rskg,skgd->rkgd", factor, block_sum, precision=EXACT)
    row_mass = jnp.einsum("rskg,skg->rkg", factor, block_mass, precision=EXACT)
    back_sum, back_peak, back_mass = send_back(
        (
            row_sum.reshape(home_total, item_total, query_width),
            row_peak.reshape(home_total, item_total, local_heads),
            row_mass.reshape(home_total, item_total, local_heads),
        )
    )
    local_ids = (sent_ids - home_first).reshape(-1)
    owned = local_ids[:, None] == jnp.arange(per_home, dtype=jnp.int32)[None, :]
    sum_rows = back_sum.reshape(-1, local_kv, group_size, HD)
    peak_rows = back_peak.reshape(-1, local_kv, group_size)
    mass_rows = back_mass.reshape(-1, local_kv, group_size)
    query_grid = home_query.reshape(per_home, local_kv, group_size, HD)
    own_score = (
        jnp.einsum("rkgd,rkd->rkg", query_grid, key_new, preferred_element_type=jnp.float32)
        * score_scale
    )
    overall = jnp.maximum(
        own_score, jnp.max(jnp.where(owned[:, :, None, None], peak_rows[:, None], NEG_FILL), axis=0)
    )
    merge_weight = jnp.where(
        owned[:, :, None, None], jnp.exp(peak_rows[:, None] - overall[None]), 0.0
    )
    own_weight = jnp.exp(own_score - overall)
    numerator = (
        jnp.einsum("prkg,pkgd->rkgd", merge_weight, sum_rows, precision=EXACT)
        + own_weight[..., None] * value_new.astype(jnp.float32)[:, :, None, :]
    )
    denominator = jnp.einsum("prkg,pkg->rkg", merge_weight, mass_rows, precision=EXACT) + own_weight
    attention = (
        (numerator / denominator[..., None]).astype(jnp.bfloat16).reshape(per_home, query_width)
    )
    partial_out = jnp.dot(
        lax.all_gather(attention, "pool", axis=0, tiled=True),
        w_out,
        preferred_element_type=jnp.float32,
    )
    head_total = lax.psum(partial_out, "tensor")
    return (resid_f + head_total).astype(jnp.bfloat16)


def solution(mesh):
    placed = (
        P("groups", "pool"),
        P("pool"),
        P("pool", "tensor"),
        P("pool", "tensor"),
        P("pool", "tensor"),
        P("tensor", "pool"),
        P(("groups", "pool"), None, "tensor"),
        P(("groups", "pool"), None, "tensor"),
        P("groups"),
        P("groups", None, None),
        P(("groups", "pool")),
        P(("groups", "pool")),
    )
    pool_count, tensor_count = mesh.shape["pool"], mesh.shape["tensor"]
    close = pool_count <= 4 and tensor_count == 4
    return jax.shard_map(
        close_pool if close else wide_pool,
        mesh=mesh,
        in_specs=placed,
        out_specs=P("groups", "pool"),
        check_vma=False,
    )
```

```python
import functools
import math

import jax
import jax.numpy as jnp
from jax import lax
from jax.experimental import pallas as pl
from jax.experimental.pallas import tpu as pltpu
from jax.sharding import PartitionSpec as P

D = 8192
HD = 128
BS = 128

EPSILON = 1e-05
THETA = 500000.0
NEG_FILL = -1e30
EXACT = lax.Precision.HIGHEST
CHUNK = 256
GROW = 128.0


def listed_at(routes, owner, row):
    per_home = routes.shape[1]
    return routes[owner, row % per_home, row // per_home]


def square_kernel(residual, out):
    resid_f = residual[...].astype(jnp.float32)
    out[...] = jnp.broadcast_to(
        jnp.sum(resid_f * resid_f, axis=1, keepdims=True), out.shape
    )


def project_kernel(pool_count, routes, residual, gain, *rest):
    squares, rest = rest[:pool_count], rest[pool_count:]
    weights, outs = rest[:3], rest[3:]
    listed = outs[0].shape[0]
    requests = residual.shape[0]
    rows = pool_count * listed
    me = lax.axis_index("pool")
    total = squares[0][...]
    for part in squares[1:]:
        total = total + part[...]
    scale = lax.rsqrt(total[:, :1] / D + EPSILON)
    resid_f = residual[...].astype(jnp.float32)
    normed = resid_f * scale * gain[...].astype(jnp.float32)[None, :]
    row_ids = lax.broadcasted_iota(jnp.int32, (rows, requests), 0)
    column_ids = lax.broadcasted_iota(jnp.int32, (rows, requests), 1)
    wanted = jnp.zeros((rows, requests), jnp.int32)
    for shift in range(pool_count):
        owner = lax.rem(me + shift, pool_count)
        for row in range(listed):
            wanted = jnp.where(
                row_ids == shift * listed + row, listed_at(routes, owner, row), wanted
            )
    pick = (column_ids == wanted).astype(jnp.float32).astype(jnp.bfloat16)
    picked = jnp.dot(
        pick, normed.astype(jnp.bfloat16), preferred_element_type=jnp.float32
    ).astype(jnp.bfloat16)
    place = 0
    for source in weights:
        for first in range(0, source.shape[1], CHUNK):
            product = jnp.dot(
                picked, source[:, first : first + CHUNK], preferred_element_type=jnp.float32
            )
            for shift in range(pool_count):
                outs[shift][:, place : place + CHUNK] = product[
                    shift * listed : (shift + 1) * listed
                ]
            place += CHUNK


def attend_kernel(
    pool_count, local_kv, group, routes, context_len, slot_route, slot_block, turn, *rest
):
    parts, (keys, values, out) = rest[:pool_count], rest[pool_count : pool_count + 3]
    turned, flat_query, flat_own, query, score, peak, mass, total = rest[pool_count + 3 :]
    listed = parts[0].shape[0]
    heads = local_kv * group
    slots = keys.shape[0]
    key_width = local_kv * HD
    homes = pool_count
    per_home = listed // homes
    score_scale = 1.0 / math.sqrt(HD)
    me = lax.axis_index("pool")
    for row in range(listed):
        turned[row : row + 1, :] = turn[pl.ds(listed_at(routes, me, row), 1), :]
    cosine, sine = turned[:, :HD], turned[:, HD:]

    def column(first):
        value = parts[1][:, first : first + HD]
        for part in parts[2:]:
            value = value + part[:, first : first + HD]
        return parts[0][:, first : first + HD] + value * (1.0 / GROW)

    def rotated(first):
        vector = column(first)
        vector = vector * cosine + pltpu.roll(vector, HD // 2, 1) * sine
        return vector.astype(jnp.bfloat16).astype(jnp.float32)

    new_keys = [rotated(k * HD) for k in range(local_kv)]
    new_values = [
        column(key_width + k * HD).astype(jnp.bfloat16).astype(jnp.float32)
        for k in range(local_kv)
    ]
    for head in range(heads):
        vector = rotated(2 * key_width + head * HD)
        own = jnp.sum(vector * new_keys[head // group], axis=1, keepdims=True) * score_scale
        flat_query[head * listed : (head + 1) * listed, :] = vector
        flat_own[head * listed : (head + 1) * listed, :] = jnp.broadcast_to(own, (listed, HD))
    lanes = lax.broadcasted_iota(jnp.int32, (heads, HD), 1)
    head_kv = lax.broadcasted_iota(jnp.int32, (heads, HD), 0) // group

    owns, mine = [], []
    peak[...] = jnp.full(peak.shape, NEG_FILL, jnp.float32)
    for row in range(listed):
        home = row // per_home
        request = listed_at(routes, me, row)
        taken = jnp.int32(0)
        for owner in range(pool_count):
            for place in range(per_home):
                same = routes[owner, place, home] == request
                taken = taken | ((owner < me) & same).astype(jnp.int32)
        vector = flat_query[pl.ds(row, heads, stride=listed), :]
        query[row] = jnp.concatenate(
            [jnp.where(head_kv == k, vector, 0.0) for k in range(local_kv)], axis=1
        ).astype(jnp.bfloat16)
        own = flat_own[pl.ds(row, heads, stride=listed), :]
        own = jnp.where(taken == 0, own, NEG_FILL)
        owns.append(own)
        mine.append(taken == 0)

    def slot_of(slot):
        entry = slot_route[slot]
        row = jnp.maximum(entry, 0)
        length = jnp.where(entry >= 0, context_len[listed_at(routes, me, row)], 0)
        return row, length - slot_block[slot] * BS

    for slot in range(slots):
        row, limit = slot_of(slot)
        value = (
            lax.dot_general(
                query[row],
                keys[slot],
                (((1,), (1,)), ((), ())),
                preferred_element_type=jnp.float32,
            )
            * score_scale
        )
        value = jnp.where(lanes < limit, value, NEG_FILL)
        score[slot] = value
        peak[row] = jnp.maximum(peak[row], value)
    for row in range(listed):
        top = jnp.maximum(jnp.max(peak[row], axis=1, keepdims=True), owns[row])
        peak[row] = top
        weight = jnp.where(mine[row], jnp.exp(owns[row] - top), 0.0)
        mass[row] = jnp.where(lanes == 0, weight, 0.0)
        fresh = jnp.zeros((heads, HD), jnp.float32)
        for k in range(local_kv):
            fresh = jnp.where(
                head_kv == k, jnp.broadcast_to(new_values[k][row : row + 1], (heads, HD)), fresh
            )
        total[row] = weight * fresh
    for slot in range(slots):
        row, limit = slot_of(slot)
        expo = jnp.where(lanes < limit, jnp.exp(score[slot] - peak[row]), 0.0)
        mass[row] += expo
        wide = jnp.dot(
            expo.astype(jnp.bfloat16), values[slot], preferred_element_type=jnp.float32
        )
        product = wide[:, :HD]
        for k in range(1, local_kv):
            product = jnp.where(head_kv == k, wide[:, k * HD : (k + 1) * HD], product)
        total[row] += product
    stats = jnp.zeros((heads, HD), jnp.float32)
    for row in range(listed):
        row_mass = jnp.sum(mass[row], axis=1, keepdims=True)
        row_peak = peak[row]
        out[row] = jnp.where(
            row_mass > 0.0, total[row] / jnp.where(row_mass > 0.0, row_mass, 1.0), 0.0
        ).astype(jnp.bfloat16)
        for first, left in ((0, row_peak), (3, row_mass)):
            for piece in range(first, first + 3):
                part = left.astype(jnp.bfloat16).astype(jnp.float32)
                stats = jnp.where(lanes == piece * listed + row, part, stats)
                left = left - part
    out[listed] = stats.astype(jnp.bfloat16)


def merge_kernel(pool_count, routes, *rest):
    parts, (w_out, out, flat) = rest[:pool_count], rest[pool_count:]
    listed = parts[0].shape[0] - 1
    heads = parts[0].shape[1]
    requests = out.shape[0]
    me = lax.axis_index("pool")
    flat[:, : requests * heads, :] = jnp.zeros((pool_count, requests * heads, HD), jnp.float32)
    lanes = lax.broadcasted_iota(jnp.int32, (heads, HD), 1)
    asked, there, peaks, masses = [], [], [], []
    for place, shift in enumerate([0, *shifts(pool_count)]):
        owner = lax.rem(me + pool_count - shift, pool_count)
        asked.append([listed_at(routes, owner, row) for row in range(listed)])
        stats = parts[place][listed].astype(jnp.float32)
        stats = (
            stats + pltpu.roll(stats, HD - listed, 1) + pltpu.roll(stats, HD - 2 * listed, 1)
        )
        source = jnp.full((heads, HD), -1, jnp.int32)
        for row, request in enumerate(asked[-1]):
            source = jnp.where(lanes == request, row, source)
        there.append(source >= 0)
        source = jnp.maximum(source, 0)
        peaks.append(
            jnp.where(there[-1], jnp.take_along_axis(stats, source, axis=1), NEG_FILL)
        )
        masses.append(jnp.take_along_axis(stats, source + 3 * listed, axis=1))
    best = functools.reduce(jnp.maximum, peaks)
    weights = [
        jnp.where(here, jnp.exp(peak - best) * mass, 0.0)
        for here, peak, mass in zip(there, peaks, masses)
    ]
    whole = sum(weights[1:], weights[0])
    whole = jnp.where(lanes < requests, whole, 1.0)
    for place, ids in enumerate(asked):
        back = jnp.zeros((heads, HD), jnp.int32)
        for row, request in enumerate(ids):
            back = jnp.where(lanes == row, request, back)
        weight = jnp.take_along_axis(weights[place] / whole, back, axis=1)
        for row, request in enumerate(ids):
            block = pl.ds(pl.multiple_of(request * heads, heads), heads)
            flat[place, block, :] = weight[:, row : row + 1] * parts[place][row].astype(
                jnp.float32
            )
    columns = []
    for head in range(heads):
        block = pl.ds(head, requests, stride=heads)
        value = flat[0, block, :]
        for place in range(1, pool_count):
            value = value + flat[place, block, :]
        columns.append(value.astype(jnp.bfloat16))
    attention = jnp.concatenate(columns, axis=1)
    for first in range(0, out.shape[1], CHUNK):
        out[:, first : first + CHUNK] = jnp.dot(
            attention, w_out[:, first : first + CHUNK], preferred_element_type=jnp.float32
        )


def shifts(pool_count):
    return range(pool_count - 1, 0, -1)


def shifted(value, axis, shift):
    count = lax.axis_size(axis)
    return lax.ppermute(value, axis, [(i, (i + shift) % count) for i in range(count)])


def pin(value):
    return pltpu.with_memory_space_constraint(value, pltpu.VMEM)


def close_pool(
    residual,
    norm_gain,
    w_query,
    w_key,
    w_value,
    w_out,
    k_cache,
    v_cache,
    context_len,
    routes,
    slot_route,
    slot_block,
):
    pool_count = lax.axis_size("pool")
    requests, depth = residual.shape
    query_width, key_width = w_query.shape[1], w_key.shape[1]
    heads, local_kv = query_width // HD, key_width // HD
    group = heads // local_kv
    listed = routes.shape[1] * routes.shape[2]
    slots = k_cache.shape[0]
    width = query_width + 2 * key_width
    routes = routes.transpose(0, 2, 1)
    in_smem = pl.BlockSpec(memory_space=pltpu.SMEM)
    in_vmem = pl.BlockSpec(memory_space=pltpu.VMEM)
    f32 = jnp.float32
    spell = pl.CostEstimate(flops=2**34, bytes_accessed=2**25, transcendentals=0)

    squares = pl.pallas_call(
        square_kernel,
        out_shape=jax.ShapeDtypeStruct((requests, HD), f32),
        in_specs=[in_vmem],
        out_specs=in_vmem,
        compiler_params=pltpu.CompilerParams(vmem_limit_bytes=4 * 2**20),
        cost_estimate=spell,
        name="square",
    )(residual)
    sent = pl.pallas_call(
        functools.partial(project_kernel, pool_count),
        out_shape=[jax.ShapeDtypeStruct((listed, width), f32)] * pool_count,
        in_specs=[in_smem] + [in_vmem] * (pool_count + 5),
        out_specs=[in_vmem] * pool_count,
        compiler_params=pltpu.CompilerParams(vmem_limit_bytes=8 * 2**20),
        cost_estimate=spell,
        name="project",
    )(
        routes,
        residual,
        norm_gain,
        squares,
        *[shifted(squares, "pool", shift) for shift in shifts(pool_count)],
        pin(w_key),
        pin(w_value),
        pin(w_query),
    )
    received = [sent[0]] + [
        shifted((sent[shift] * GROW).astype(jnp.float16), "pool", shift).astype(f32)
        for shift in shifts(pool_count)
    ]
    frequencies = THETA ** (-2.0 * jnp.arange(HD // 2, dtype=f32) / HD)
    late_len, _ = lax.optimization_barrier((context_len, sent[0]))
    angles = late_len.astype(f32)[:, None] * frequencies[None, :]
    cosine, sine = jnp.cos(angles), jnp.sin(angles)
    turn = jnp.concatenate([cosine, cosine, -sine, sine], axis=1)
    partial = pl.pallas_call(
        functools.partial(attend_kernel, pool_count, local_kv, group),
        out_shape=jax.ShapeDtypeStruct((listed + 1, heads, HD), jnp.bfloat16),
        in_specs=[in_smem] * 4 + [in_vmem] * (pool_count + 3),
        out_specs=in_vmem,
        scratch_shapes=[
            pltpu.VMEM((listed, 2 * HD), f32),
            pltpu.VMEM(((heads + 1) * listed, HD), f32),
            pltpu.VMEM(((heads + 1) * listed, HD), f32),
            pltpu.VMEM((listed, heads, key_width), jnp.bfloat16),
            pltpu.VMEM((slots, heads, HD), f32),
            pltpu.VMEM((listed, heads, HD), f32),
            pltpu.VMEM((listed, heads, HD), f32),
            pltpu.VMEM((listed, heads, HD), f32),
        ],
        compiler_params=pltpu.CompilerParams(vmem_limit_bytes=8 * 2**20),
        cost_estimate=spell,
        name="attend",
    )(routes, context_len, slot_route, slot_block, turn, *received, pin(k_cache), pin(v_cache))
    partials = [partial] + [shifted(partial, "pool", shift) for shift in shifts(pool_count)]

    product = pl.pallas_call(
        functools.partial(merge_kernel, pool_count),
        out_shape=jax.ShapeDtypeStruct((requests, w_out.shape[1]), f32),
        in_specs=[in_smem] + [in_vmem] * (pool_count + 1),
        out_specs=in_vmem,
        scratch_shapes=[pltpu.VMEM((pool_count, (requests + 1) * heads, HD), f32)],
        compiler_params=pltpu.CompilerParams(vmem_limit_bytes=8 * 2**20),
        cost_estimate=spell,
        name="merge",
    )(routes, *partials, pin(w_out))
    tensor_count = lax.axis_size("tensor")
    product = product.astype(jnp.bfloat16)
    one, two, three = [
        lax.ppermute(product, "tensor", [(i, i ^ d) for i in range(tensor_count)]).astype(f32)
        for d in (1, 2, 3)
    ]
    product = product.astype(f32)
    return (residual.astype(f32) + ((product + one) + (two + three))).astype(jnp.bfloat16)


def rotate(vectors, positions):
    half_dim = vectors.shape[-1] // 2
    frequencies = THETA ** (-2.0 * jnp.arange(half_dim, dtype=jnp.float32) / vectors.shape[-1])
    angles = positions.astype(jnp.float32)[:, None] * frequencies[None, :]
    cosine = jnp.cos(angles)[:, None, :]
    sine_part = jnp.sin(angles)[:, None, :]
    first_half = vectors[..., :half_dim]
    second_half = vectors[..., half_dim:]
    return jnp.concatenate(
        [
            first_half * cosine - second_half * sine_part,
            second_half * cosine + first_half * sine_part,
        ],
        axis=-1,
    )


def send_back(parts):
    return (
        lax.all_to_all(parts[0], "pool", split_axis=0, concat_axis=0, tiled=True),
        lax.all_to_all(parts[1], "pool", split_axis=0, concat_axis=0, tiled=True),
        lax.all_to_all(parts[2], "pool", split_axis=0, concat_axis=0, tiled=True),
    )


def wide_pool(
    residual,
    norm_gain,
    w_query,
    w_key,
    w_value,
    w_out,
    k_cache,
    v_cache,
    context_len,
    routes,
    slot_route,
    slot_block,
):
    pool_count = lax.axis_size("pool")
    pool_index = lax.axis_index("pool")
    request_count = residual.shape[0]
    per_home = request_count // pool_count
    home_first = pool_index * per_home
    query_width = w_query.shape[1]
    key_width = w_key.shape[1]
    local_heads = query_width // HD
    local_kv = key_width // HD
    group_size = local_heads // local_kv
    slot_count = k_cache.shape[0]
    score_scale = 1.0 / math.sqrt(HD)
    resid_f = residual.astype(jnp.float32)
    square_total = lax.psum(jnp.sum(resid_f * resid_f, axis=1), "pool")
    normed = (
        resid_f
        * lax.rsqrt(square_total / D + EPSILON)[:, None]
        * norm_gain.astype(jnp.float32)[None, :]
    ).astype(jnp.bfloat16)
    owner_routes = lax.dynamic_slice_in_dim(routes, pool_index, 1, 0)[0].reshape(-1)
    slot_request = jnp.where(slot_route >= 0, owner_routes[jnp.maximum(slot_route, 0)], -1)
    key_blocks = k_cache.reshape(slot_count, BS, local_kv, HD)
    value_blocks = v_cache.reshape(slot_count, BS, local_kv, HD)
    positions = slot_block[:, None] * BS + jnp.arange(BS, dtype=jnp.int32)[None, :]
    sent_ids = lax.dynamic_slice_in_dim(routes, pool_index, 1, 1)[:, 0, :]
    home_rows = lax.psum_scatter(
        jnp.concatenate(
            [
                jnp.dot(normed, w_query, preferred_element_type=jnp.float32),
                jnp.dot(normed, w_key, preferred_element_type=jnp.float32),
                jnp.dot(normed, w_value, preferred_element_type=jnp.float32),
            ],
            axis=1,
        ),
        "pool",
        scatter_dimension=0,
        tiled=True,
    )
    home_len = lax.dynamic_slice_in_dim(context_len, home_first, per_home, 0)
    row_total = home_rows.shape[0]
    query = rotate(home_rows[:, :query_width].reshape(row_total, local_heads, HD), home_len).astype(
        jnp.bfloat16
    )
    key_new = rotate(
        home_rows[:, query_width : query_width + key_width].reshape(row_total, local_kv, HD),
        home_len,
    ).astype(jnp.bfloat16)
    value_new = (
        home_rows[:, query_width + key_width :]
        .astype(jnp.bfloat16)
        .reshape(row_total, local_kv, HD)
    )
    home_query = query.reshape(row_total, query_width)
    sent_query = home_query[sent_ids - home_first]
    sent_info = jnp.stack([sent_ids, context_len[sent_ids]], axis=-1)
    rows_query = lax.all_to_all(sent_query, "pool", split_axis=0, concat_axis=0, tiled=True)
    rows_info = lax.all_to_all(sent_info, "pool", split_axis=0, concat_axis=0, tiled=True)
    home_total = rows_query.shape[0]
    item_total = rows_query.shape[1]
    flat_query = rows_query.reshape(home_total * item_total, query_width)
    flat_ids = rows_info[..., 0].reshape(-1)
    flat_len = rows_info[..., 1].reshape(-1)
    matches = slot_request[:, None] == flat_ids[None, :]
    slot_query = jnp.dot(
        matches.astype(jnp.bfloat16), flat_query, preferred_element_type=jnp.float32
    ).astype(jnp.bfloat16)
    grouped = slot_query.reshape(slot_count, local_kv, group_size, HD)
    slot_len = jnp.sum(jnp.where(matches, flat_len[None, :], 0), axis=1)
    present = jnp.any(matches, axis=1)
    in_range = present[:, None] & (positions < slot_len[:, None])
    valid_mask = in_range[:, None, None, :]
    scores = (
        jnp.einsum("skgd,sbkd->skgb", grouped, key_blocks, preferred_element_type=jnp.float32)
        * score_scale
    )
    block_peak = jnp.max(jnp.where(valid_mask, scores, NEG_FILL), axis=3)
    exponent = jnp.exp(jnp.where(valid_mask, scores - block_peak[..., None], NEG_FILL))
    weights = exponent.astype(jnp.bfloat16)
    block_sum = jnp.einsum(
        "skgb,sbkd->skgd", weights, value_blocks, preferred_element_type=jnp.float32
    )
    block_mass = jnp.sum(exponent, axis=3)
    hits = matches.T
    row_peak = jnp.max(jnp.where(hits[:, :, None, None], block_peak[None], NEG_FILL), axis=1)
    factor = jnp.where(hits[:, :, None, None], jnp.exp(block_peak[None] - row_peak[:, None]), 0.0)
    row_sum = jnp.einsum("rskg,skgd->rkgd", factor, block_sum, precision=EXACT)
    row_mass = jnp.einsum("rskg,skg->rkg", factor, block_mass, precision=EXACT)
    back_sum, back_peak, back_mass = send_back(
        (
            row_sum.reshape(home_total, item_total, query_width),
            row_peak.reshape(home_total, item_total, local_heads),
            row_mass.reshape(home_total, item_total, local_heads),
        )
    )
    local_ids = (sent_ids - home_first).reshape(-1)
    owned = local_ids[:, None] == jnp.arange(per_home, dtype=jnp.int32)[None, :]
    sum_rows = back_sum.reshape(-1, local_kv, group_size, HD)
    peak_rows = back_peak.reshape(-1, local_kv, group_size)
    mass_rows = back_mass.reshape(-1, local_kv, group_size)
    query_grid = home_query.reshape(per_home, local_kv, group_size, HD)
    own_score = (
        jnp.einsum("rkgd,rkd->rkg", query_grid, key_new, preferred_element_type=jnp.float32)
        * score_scale
    )
    overall = jnp.maximum(
        own_score, jnp.max(jnp.where(owned[:, :, None, None], peak_rows[:, None], NEG_FILL), axis=0)
    )
    merge_weight = jnp.where(
        owned[:, :, None, None], jnp.exp(peak_rows[:, None] - overall[None]), 0.0
    )
    own_weight = jnp.exp(own_score - overall)
    numerator = (
        jnp.einsum("prkg,pkgd->rkgd", merge_weight, sum_rows, precision=EXACT)
        + own_weight[..., None] * value_new.astype(jnp.float32)[:, :, None, :]
    )
    denominator = jnp.einsum("prkg,pkg->rkg", merge_weight, mass_rows, precision=EXACT) + own_weight
    attention = (
        (numerator / denominator[..., None]).astype(jnp.bfloat16).reshape(per_home, query_width)
    )
    partial_out = jnp.dot(
        lax.all_gather(attention, "pool", axis=0, tiled=True),
        w_out,
        preferred_element_type=jnp.float32,
    )
    head_total = lax.psum(partial_out, "tensor")
    return (resid_f + head_total).astype(jnp.bfloat16)


def solution(mesh):
    placed = (
        P("groups", "pool"),
        P("pool"),
        P("pool", "tensor"),
        P("pool", "tensor"),
        P("pool", "tensor"),
        P("tensor", "pool"),
        P(("groups", "pool"), None, "tensor"),
        P(("groups", "pool"), None, "tensor"),
        P("groups"),
        P("groups", None, None),
        P(("groups", "pool")),
        P(("groups", "pool")),
    )
    pool_count, tensor_count = mesh.shape["pool"], mesh.shape["tensor"]
    close = pool_count <= 4 and tensor_count == 4
    return jax.shard_map(
        close_pool if close else wide_pool,
        mesh=mesh,
        in_specs=placed,
        out_specs=P("groups", "pool"),
        check_vma=False,
    )
```

```python
import functools
import math

import jax
import jax.numpy as jnp
from jax import lax
from jax.experimental import pallas as pl
from jax.experimental.pallas import tpu as pltpu
from jax.sharding import PartitionSpec as P

D = 8192
HD = 128
BS = 128

EPSILON = 1e-05
THETA = 500000.0
NEG_FILL = -1e30
EXACT = lax.Precision.HIGHEST
CHUNK = 256
GROW = 128.0


def listed_at(routes, owner, row):
    per_home = routes.shape[1]
    return routes[owner, row % per_home, row // per_home]


def square_kernel(residual, out):
    resid_f = residual[...].astype(jnp.float32)
    out[...] = jnp.broadcast_to(
        jnp.sum(resid_f * resid_f, axis=1, keepdims=True), out.shape
    )


def pick_kernel(pool_count, listed, routes, residual, after, out, pick):
    requests = residual.shape[0]
    rows = pool_count * listed
    me = lax.axis_index("pool")
    row_ids = lax.broadcasted_iota(jnp.int32, (rows, HD), 0)
    wanted = jnp.zeros((rows, HD), jnp.int32)
    for shift in range(pool_count):
        owner = lax.rem(me + shift, pool_count)
        for row in range(listed):
            wanted = jnp.where(
                row_ids == shift * listed + row, listed_at(routes, owner, row), wanted
            )
    chosen = (lax.broadcasted_iota(jnp.int32, (rows, HD), 1) == wanted).astype(jnp.float32)
    pick[...] = chosen
    out[...] = jnp.dot(
        chosen[:, :requests].astype(jnp.bfloat16),
        residual[...],
        preferred_element_type=jnp.float32,
    )


def project_kernel(pool_count, residual, pick, gain, *rest):
    squares, rest = rest[:pool_count], rest[pool_count:]
    weights, outs = rest[:3], rest[3:]
    listed = outs[0].shape[0]
    total = squares[0][...]
    for part in squares[1:]:
        total = total + part[...]
    ids = [lax.broadcasted_iota(jnp.int32, total.shape, axis) for axis in range(2)]
    scale = jnp.where(ids[0] == ids[1], lax.rsqrt(total / D + EPSILON), 0.0)
    scale = jnp.sum(scale, axis=0, keepdims=True)
    scale = jnp.sum(pick[...] * scale, axis=1, keepdims=True)
    normed = residual[...] * scale * gain[...].astype(jnp.float32)[None, :]
    picked = normed.astype(jnp.bfloat16)
    place = 0
    for source in weights:
        for first in range(0, source.shape[1], CHUNK):
            product = jnp.dot(
                picked, source[:, first : first + CHUNK], preferred_element_type=jnp.float32
            )
            for shift in range(pool_count):
                outs[shift][:, place : place + CHUNK] = product[
                    shift * listed : (shift + 1) * listed
                ]
            place += CHUNK


def attend_kernel(
    pool_count, local_kv, group, routes, context_len, slot_route, slot_block, turn, *rest
):
    parts, (keys, values, out) = rest[:pool_count], rest[pool_count : pool_count + 3]
    turned, flat_query, flat_own, query, score, peak, mass, total = rest[pool_count + 3 :]
    listed = parts[0].shape[0]
    heads = local_kv * group
    slots = keys.shape[0]
    key_width = local_kv * HD
    homes = pool_count
    per_home = listed // homes
    score_scale = 1.0 / math.sqrt(HD)
    me = lax.axis_index("pool")
    for row in range(listed):
        turned[row : row + 1, :] = turn[pl.ds(listed_at(routes, me, row), 1), :]
    cosine, sine = turned[:, :HD], turned[:, HD:]

    def column(first):
        value = parts[1][:, first : first + HD]
        for part in parts[2:]:
            value = value + part[:, first : first + HD]
        return parts[0][:, first : first + HD] + value * (1.0 / GROW)

    def rotated(first):
        vector = column(first)
        vector = vector * cosine + pltpu.roll(vector, HD // 2, 1) * sine
        return vector.astype(jnp.bfloat16).astype(jnp.float32)

    new_keys = [rotated(k * HD) for k in range(local_kv)]
    new_values = [
        column(key_width + k * HD).astype(jnp.bfloat16).astype(jnp.float32)
        for k in range(local_kv)
    ]
    for head in range(heads):
        vector = rotated(2 * key_width + head * HD)
        own = jnp.sum(vector * new_keys[head // group], axis=1, keepdims=True) * score_scale
        flat_query[head * listed : (head + 1) * listed, :] = vector
        flat_own[head * listed : (head + 1) * listed, :] = jnp.broadcast_to(own, (listed, HD))
    lanes = lax.broadcasted_iota(jnp.int32, (heads, HD), 1)
    head_kv = lax.broadcasted_iota(jnp.int32, (heads, HD), 0) // group

    owns, mine = [], []
    peak[...] = jnp.full(peak.shape, NEG_FILL, jnp.float32)
    for row in range(listed):
        home = row // per_home
        request = listed_at(routes, me, row)
        taken = jnp.int32(0)
        for owner in range(pool_count):
            for place in range(per_home):
                same = routes[owner, place, home] == request
                taken = taken | ((owner < me) & same).astype(jnp.int32)
        vector = flat_query[pl.ds(row, heads, stride=listed), :]
        query[row] = jnp.concatenate(
            [jnp.where(head_kv == k, vector, 0.0) for k in range(local_kv)], axis=1
        ).astype(jnp.bfloat16)
        own = flat_own[pl.ds(row, heads, stride=listed), :]
        own = jnp.where(taken == 0, own, NEG_FILL)
        owns.append(own)
        mine.append(taken == 0)

    def slot_of(slot):
        entry = slot_route[slot]
        row = jnp.maximum(entry, 0)
        length = jnp.where(entry >= 0, context_len[listed_at(routes, me, row)], 0)
        return row, length - slot_block[slot] * BS

    for slot in range(slots):
        row, limit = slot_of(slot)
        value = (
            lax.dot_general(
                query[row],
                keys[slot],
                (((1,), (1,)), ((), ())),
                preferred_element_type=jnp.float32,
            )
            * score_scale
        )
        value = jnp.where(lanes < limit, value, NEG_FILL)
        score[slot] = value
        peak[row] = jnp.maximum(peak[row], value)
    for row in range(listed):
        top = jnp.maximum(jnp.max(peak[row], axis=1, keepdims=True), owns[row])
        peak[row] = top
        weight = jnp.where(mine[row], jnp.exp(owns[row] - top), 0.0)
        mass[row] = jnp.where(lanes == 0, weight, 0.0)
        fresh = jnp.zeros((heads, HD), jnp.float32)
        for k in range(local_kv):
            fresh = jnp.where(
                head_kv == k, jnp.broadcast_to(new_values[k][row : row + 1], (heads, HD)), fresh
            )
        total[row] = weight * fresh
    for slot in range(slots):
        row, limit = slot_of(slot)
        expo = jnp.where(lanes < limit, jnp.exp(score[slot] - peak[row]), 0.0)
        mass[row] += expo
        wide = jnp.dot(
            expo.astype(jnp.bfloat16), values[slot], preferred_element_type=jnp.float32
        )
        product = wide[:, :HD]
        for k in range(1, local_kv):
            product = jnp.where(head_kv == k, wide[:, k * HD : (k + 1) * HD], product)
        total[row] += product
    stats = jnp.zeros((heads, HD), jnp.float32)
    for row in range(listed):
        row_mass = jnp.sum(mass[row], axis=1, keepdims=True)
        row_peak = peak[row]
        out[row] = jnp.where(
            row_mass > 0.0, total[row] / jnp.where(row_mass > 0.0, row_mass, 1.0), 0.0
        ).astype(jnp.bfloat16)
        for first, left in ((0, row_peak), (3, row_mass)):
            for piece in range(first, first + 3):
                part = left.astype(jnp.bfloat16).astype(jnp.float32)
                stats = jnp.where(lanes == piece * listed + row, part, stats)
                left = left - part
    out[listed] = stats.astype(jnp.bfloat16)


def merge_kernel(pool_count, routes, *rest):
    parts, (w_out, out, flat) = rest[:pool_count], rest[pool_count:]
    listed = parts[0].shape[0] - 1
    heads = parts[0].shape[1]
    requests = out.shape[0]
    me = lax.axis_index("pool")
    flat[:, : requests * heads, :] = jnp.zeros((pool_count, requests * heads, HD), jnp.float32)
    lanes = lax.broadcasted_iota(jnp.int32, (heads, HD), 1)
    asked, there, peaks, masses = [], [], [], []
    for place, shift in enumerate([0, *shifts(pool_count)]):
        owner = lax.rem(me + pool_count - shift, pool_count)
        asked.append([listed_at(routes, owner, row) for row in range(listed)])
        stats = parts[place][listed].astype(jnp.float32)
        stats = (
            stats + pltpu.roll(stats, HD - listed, 1) + pltpu.roll(stats, HD - 2 * listed, 1)
        )
        source = jnp.full((heads, HD), -1, jnp.int32)
        for row, request in enumerate(asked[-1]):
            source = jnp.where(lanes == request, row, source)
        there.append(source >= 0)
        source = jnp.maximum(source, 0)
        peaks.append(
            jnp.where(there[-1], jnp.take_along_axis(stats, source, axis=1), NEG_FILL)
        )
        masses.append(jnp.take_along_axis(stats, source + 3 * listed, axis=1))
    best = functools.reduce(jnp.maximum, peaks)
    weights = [
        jnp.where(here, jnp.exp(peak - best) * mass, 0.0)
        for here, peak, mass in zip(there, peaks, masses)
    ]
    whole = sum(weights[1:], weights[0])
    whole = jnp.where(lanes < requests, whole, 1.0)
    for place, ids in enumerate(asked):
        back = jnp.zeros((heads, HD), jnp.int32)
        for row, request in enumerate(ids):
            back = jnp.where(lanes == row, request, back)
        weight = jnp.take_along_axis(weights[place] / whole, back, axis=1)
        for row, request in enumerate(ids):
            block = pl.ds(pl.multiple_of(request * heads, heads), heads)
            flat[place, block, :] = weight[:, row : row + 1] * parts[place][row].astype(
                jnp.float32
            )
    columns = []
    for head in range(heads):
        block = pl.ds(head, requests, stride=heads)
        value = flat[0, block, :]
        for place in range(1, pool_count):
            value = value + flat[place, block, :]
        columns.append(value.astype(jnp.bfloat16))
    attention = jnp.concatenate(columns, axis=1)
    for first in range(0, out.shape[1], CHUNK):
        out[:, first : first + CHUNK] = jnp.dot(
            attention, w_out[:, first : first + CHUNK], preferred_element_type=jnp.float32
        )


def shifts(pool_count):
    return range(1, pool_count)


def shifted(value, axis, shift):
    count = lax.axis_size(axis)
    return lax.ppermute(value, axis, [(i, (i + shift) % count) for i in range(count)])


def pin(value):
    return pltpu.with_memory_space_constraint(value, pltpu.VMEM)


def close_pool(
    residual,
    norm_gain,
    w_query,
    w_key,
    w_value,
    w_out,
    k_cache,
    v_cache,
    context_len,
    routes,
    slot_route,
    slot_block,
):
    pool_count = lax.axis_size("pool")
    requests, depth = residual.shape
    query_width, key_width = w_query.shape[1], w_key.shape[1]
    heads, local_kv = query_width // HD, key_width // HD
    group = heads // local_kv
    listed = routes.shape[1] * routes.shape[2]
    slots = k_cache.shape[0]
    width = query_width + 2 * key_width
    routes = routes.transpose(0, 2, 1)
    in_smem = pl.BlockSpec(memory_space=pltpu.SMEM)
    in_vmem = pl.BlockSpec(memory_space=pltpu.VMEM)
    f32 = jnp.float32
    spell = pl.CostEstimate(flops=2**34, bytes_accessed=2**25, transcendentals=0)

    squares = pl.pallas_call(
        square_kernel,
        out_shape=jax.ShapeDtypeStruct((requests, HD), f32),
        in_specs=[in_vmem],
        out_specs=in_vmem,
        compiler_params=pltpu.CompilerParams(vmem_limit_bytes=4 * 2**20),
        cost_estimate=spell,
        name="square",
    )(residual)
    rows = pool_count * listed
    picked, pick = pl.pallas_call(
        functools.partial(pick_kernel, pool_count, listed),
        out_shape=[
            jax.ShapeDtypeStruct((rows, depth), f32),
            jax.ShapeDtypeStruct((rows, HD), f32),
        ],
        in_specs=[in_smem, in_vmem, in_vmem],
        out_specs=[in_vmem] * 2,
        compiler_params=pltpu.CompilerParams(vmem_limit_bytes=4 * 2**20),
        cost_estimate=spell,
        name="pick",
    )(routes, residual, squares)
    sent = pl.pallas_call(
        functools.partial(project_kernel, pool_count),
        out_shape=[jax.ShapeDtypeStruct((listed, width), f32)] * pool_count,
        in_specs=[in_vmem] * (pool_count + 6),
        out_specs=[in_vmem] * pool_count,
        compiler_params=pltpu.CompilerParams(vmem_limit_bytes=8 * 2**20),
        cost_estimate=spell,
        name="project",
    )(
        picked,
        pick,
        norm_gain,
        squares,
        *[shifted(squares, "pool", shift) for shift in range(1, pool_count)],
        pin(w_key),
        pin(w_value),
        pin(w_query),
    )
    received = [sent[0]] + [
        shifted((sent[shift] * GROW).astype(jnp.float16), "pool", shift).astype(f32)
        for shift in shifts(pool_count)
    ]
    frequencies = THETA ** (-2.0 * jnp.arange(HD // 2, dtype=f32) / HD)
    late_len, _ = lax.optimization_barrier((context_len, sent[0]))
    angles = late_len.astype(f32)[:, None] * frequencies[None, :]
    cosine, sine = jnp.cos(angles), jnp.sin(angles)
    turn = jnp.concatenate([cosine, cosine, -sine, sine], axis=1)
    partial = pl.pallas_call(
        functools.partial(attend_kernel, pool_count, local_kv, group),
        out_shape=jax.ShapeDtypeStruct((listed + 1, heads, HD), jnp.bfloat16),
        in_specs=[in_smem] * 4 + [in_vmem] * (pool_count + 3),
        out_specs=in_vmem,
        scratch_shapes=[
            pltpu.VMEM((listed, 2 * HD), f32),
            pltpu.VMEM(((heads + 1) * listed, HD), f32),
            pltpu.VMEM(((heads + 1) * listed, HD), f32),
            pltpu.VMEM((listed, heads, key_width), jnp.bfloat16),
            pltpu.VMEM((slots, heads, HD), f32),
            pltpu.VMEM((listed, heads, HD), f32),
            pltpu.VMEM((listed, heads, HD), f32),
            pltpu.VMEM((listed, heads, HD), f32),
        ],
        compiler_params=pltpu.CompilerParams(vmem_limit_bytes=8 * 2**20),
        cost_estimate=spell,
        name="attend",
    )(routes, context_len, slot_route, slot_block, turn, *received, pin(k_cache), pin(v_cache))
    partials = [partial] + [shifted(partial, "pool", shift) for shift in shifts(pool_count)]

    product = pl.pallas_call(
        functools.partial(merge_kernel, pool_count),
        out_shape=jax.ShapeDtypeStruct((requests, w_out.shape[1]), f32),
        in_specs=[in_smem] + [in_vmem] * (pool_count + 1),
        out_specs=in_vmem,
        scratch_shapes=[pltpu.VMEM((pool_count, (requests + 1) * heads, HD), f32)],
        compiler_params=pltpu.CompilerParams(vmem_limit_bytes=8 * 2**20),
        cost_estimate=spell,
        name="merge",
    )(routes, *partials, pin(w_out))
    tensor_count = lax.axis_size("tensor")
    product = product.astype(jnp.bfloat16)
    one, two, three = [
        lax.ppermute(product, "tensor", [(i, i ^ d) for i in range(tensor_count)]).astype(f32)
        for d in (1, 2, 3)
    ]
    product = product.astype(f32)
    return (residual.astype(f32) + ((product + one) + (two + three))).astype(jnp.bfloat16)


def rotate(vectors, positions):
    half_dim = vectors.shape[-1] // 2
    frequencies = THETA ** (-2.0 * jnp.arange(half_dim, dtype=jnp.float32) / vectors.shape[-1])
    angles = positions.astype(jnp.float32)[:, None] * frequencies[None, :]
    cosine = jnp.cos(angles)[:, None, :]
    sine_part = jnp.sin(angles)[:, None, :]
    first_half = vectors[..., :half_dim]
    second_half = vectors[..., half_dim:]
    return jnp.concatenate(
        [
            first_half * cosine - second_half * sine_part,
            second_half * cosine + first_half * sine_part,
        ],
        axis=-1,
    )


def send_back(parts):
    return (
        lax.all_to_all(parts[0], "pool", split_axis=0, concat_axis=0, tiled=True),
        lax.all_to_all(parts[1], "pool", split_axis=0, concat_axis=0, tiled=True),
        lax.all_to_all(parts[2], "pool", split_axis=0, concat_axis=0, tiled=True),
    )


def wide_pool(
    residual,
    norm_gain,
    w_query,
    w_key,
    w_value,
    w_out,
    k_cache,
    v_cache,
    context_len,
    routes,
    slot_route,
    slot_block,
):
    pool_count = lax.axis_size("pool")
    pool_index = lax.axis_index("pool")
    request_count = residual.shape[0]
    per_home = request_count // pool_count
    home_first = pool_index * per_home
    query_width = w_query.shape[1]
    key_width = w_key.shape[1]
    local_heads = query_width // HD
    local_kv = key_width // HD
    group_size = local_heads // local_kv
    slot_count = k_cache.shape[0]
    score_scale = 1.0 / math.sqrt(HD)
    resid_f = residual.astype(jnp.float32)
    square_total = lax.psum(jnp.sum(resid_f * resid_f, axis=1), "pool")
    normed = (
        resid_f
        * lax.rsqrt(square_total / D + EPSILON)[:, None]
        * norm_gain.astype(jnp.float32)[None, :]
    ).astype(jnp.bfloat16)
    owner_routes = lax.dynamic_slice_in_dim(routes, pool_index, 1, 0)[0].reshape(-1)
    slot_request = jnp.where(slot_route >= 0, owner_routes[jnp.maximum(slot_route, 0)], -1)
    key_blocks = k_cache.reshape(slot_count, BS, local_kv, HD)
    value_blocks = v_cache.reshape(slot_count, BS, local_kv, HD)
    positions = slot_block[:, None] * BS + jnp.arange(BS, dtype=jnp.int32)[None, :]
    sent_ids = lax.dynamic_slice_in_dim(routes, pool_index, 1, 1)[:, 0, :]
    home_rows = lax.psum_scatter(
        jnp.concatenate(
            [
                jnp.dot(normed, w_query, preferred_element_type=jnp.float32),
                jnp.dot(normed, w_key, preferred_element_type=jnp.float32),
                jnp.dot(normed, w_value, preferred_element_type=jnp.float32),
            ],
            axis=1,
        ),
        "pool",
        scatter_dimension=0,
        tiled=True,
    )
    home_len = lax.dynamic_slice_in_dim(context_len, home_first, per_home, 0)
    row_total = home_rows.shape[0]
    query = rotate(home_rows[:, :query_width].reshape(row_total, local_heads, HD), home_len).astype(
        jnp.bfloat16
    )
    key_new = rotate(
        home_rows[:, query_width : query_width + key_width].reshape(row_total, local_kv, HD),
        home_len,
    ).astype(jnp.bfloat16)
    value_new = (
        home_rows[:, query_width + key_width :]
        .astype(jnp.bfloat16)
        .reshape(row_total, local_kv, HD)
    )
    home_query = query.reshape(row_total, query_width)
    sent_query = home_query[sent_ids - home_first]
    sent_info = jnp.stack([sent_ids, context_len[sent_ids]], axis=-1)
    rows_query = lax.all_to_all(sent_query, "pool", split_axis=0, concat_axis=0, tiled=True)
    rows_info = lax.all_to_all(sent_info, "pool", split_axis=0, concat_axis=0, tiled=True)
    home_total = rows_query.shape[0]
    item_total = rows_query.shape[1]
    flat_query = rows_query.reshape(home_total * item_total, query_width)
    flat_ids = rows_info[..., 0].reshape(-1)
    flat_len = rows_info[..., 1].reshape(-1)
    matches = slot_request[:, None] == flat_ids[None, :]
    slot_query = jnp.dot(
        matches.astype(jnp.bfloat16), flat_query, preferred_element_type=jnp.float32
    ).astype(jnp.bfloat16)
    grouped = slot_query.reshape(slot_count, local_kv, group_size, HD)
    slot_len = jnp.sum(jnp.where(matches, flat_len[None, :], 0), axis=1)
    present = jnp.any(matches, axis=1)
    in_range = present[:, None] & (positions < slot_len[:, None])
    valid_mask = in_range[:, None, None, :]
    scores = (
        jnp.einsum("skgd,sbkd->skgb", grouped, key_blocks, preferred_element_type=jnp.float32)
        * score_scale
    )
    block_peak = jnp.max(jnp.where(valid_mask, scores, NEG_FILL), axis=3)
    exponent = jnp.exp(jnp.where(valid_mask, scores - block_peak[..., None], NEG_FILL))
    weights = exponent.astype(jnp.bfloat16)
    block_sum = jnp.einsum(
        "skgb,sbkd->skgd", weights, value_blocks, preferred_element_type=jnp.float32
    )
    block_mass = jnp.sum(exponent, axis=3)
    hits = matches.T
    row_peak = jnp.max(jnp.where(hits[:, :, None, None], block_peak[None], NEG_FILL), axis=1)
    factor = jnp.where(hits[:, :, None, None], jnp.exp(block_peak[None] - row_peak[:, None]), 0.0)
    row_sum = jnp.einsum("rskg,skgd->rkgd", factor, block_sum, precision=EXACT)
    row_mass = jnp.einsum("rskg,skg->rkg", factor, block_mass, precision=EXACT)
    back_sum, back_peak, back_mass = send_back(
        (
            row_sum.reshape(home_total, item_total, query_width),
            row_peak.reshape(home_total, item_total, local_heads),
            row_mass.reshape(home_total, item_total, local_heads),
        )
    )
    local_ids = (sent_ids - home_first).reshape(-1)
    owned = local_ids[:, None] == jnp.arange(per_home, dtype=jnp.int32)[None, :]
    sum_rows = back_sum.reshape(-1, local_kv, group_size, HD)
    peak_rows = back_peak.reshape(-1, local_kv, group_size)
    mass_rows = back_mass.reshape(-1, local_kv, group_size)
    query_grid = home_query.reshape(per_home, local_kv, group_size, HD)
    own_score = (
        jnp.einsum("rkgd,rkd->rkg", query_grid, key_new, preferred_element_type=jnp.float32)
        * score_scale
    )
    overall = jnp.maximum(
        own_score, jnp.max(jnp.where(owned[:, :, None, None], peak_rows[:, None], NEG_FILL), axis=0)
    )
    merge_weight = jnp.where(
        owned[:, :, None, None], jnp.exp(peak_rows[:, None] - overall[None]), 0.0
    )
    own_weight = jnp.exp(own_score - overall)
    numerator = (
        jnp.einsum("prkg,pkgd->rkgd", merge_weight, sum_rows, precision=EXACT)
        + own_weight[..., None] * value_new.astype(jnp.float32)[:, :, None, :]
    )
    denominator = jnp.einsum("prkg,pkg->rkg", merge_weight, mass_rows, precision=EXACT) + own_weight
    attention = (
        (numerator / denominator[..., None]).astype(jnp.bfloat16).reshape(per_home, query_width)
    )
    partial_out = jnp.dot(
        lax.all_gather(attention, "pool", axis=0, tiled=True),
        w_out,
        preferred_element_type=jnp.float32,
    )
    head_total = lax.psum(partial_out, "tensor")
    return (resid_f + head_total).astype(jnp.bfloat16)


def solution(mesh):
    placed = (
        P("groups", "pool"),
        P("pool"),
        P("pool", "tensor"),
        P("pool", "tensor"),
        P("pool", "tensor"),
        P("tensor", "pool"),
        P(("groups", "pool"), None, "tensor"),
        P(("groups", "pool"), None, "tensor"),
        P("groups"),
        P("groups", None, None),
        P(("groups", "pool")),
        P(("groups", "pool")),
    )
    pool_count, tensor_count = mesh.shape["pool"], mesh.shape["tensor"]
    close = pool_count <= 4 and tensor_count == 4
    return jax.shard_map(
        close_pool if close else wide_pool,
        mesh=mesh,
        in_specs=placed,
        out_specs=P("groups", "pool"),
        check_vma=False,
    )
```

```python
import functools
import math

import jax
import jax.numpy as jnp
from jax import lax
from jax.experimental import pallas as pl
from jax.experimental.pallas import tpu as pltpu
from jax.sharding import PartitionSpec as P

D = 8192
HD = 128
BS = 128

EPSILON = 1e-05
THETA = 500000.0
NEG_FILL = -1e30
EXACT = lax.Precision.HIGHEST
CHUNK = 256
GROW = 128.0


def listed_at(routes, owner, row):
    per_home = routes.shape[1]
    return routes[owner, row % per_home, row // per_home]


def square_kernel(residual, out):
    resid_f = residual[...].astype(jnp.float32)
    out[...] = jnp.broadcast_to(
        jnp.sum(resid_f * resid_f, axis=1, keepdims=True), out.shape
    )


def pick_kernel(pool_count, listed, routes, residual, after, out, pick):
    requests = residual.shape[0]
    rows = pool_count * listed
    me = lax.axis_index("pool")
    row_ids = lax.broadcasted_iota(jnp.int32, (rows, HD), 0)
    wanted = jnp.zeros((rows, HD), jnp.int32)
    for shift in range(pool_count):
        owner = lax.rem(me + shift, pool_count)
        for row in range(listed):
            wanted = jnp.where(
                row_ids == shift * listed + row, listed_at(routes, owner, row), wanted
            )
    chosen = (lax.broadcasted_iota(jnp.int32, (rows, HD), 1) == wanted).astype(jnp.float32)
    pick[...] = chosen
    out[...] = jnp.dot(
        chosen[:, :requests].astype(jnp.bfloat16),
        residual[...],
        preferred_element_type=jnp.float32,
    )


def project_kernel(pool_count, residual, pick, gain, *rest):
    squares, rest = rest[:pool_count], rest[pool_count:]
    weights, outs = rest[:3], rest[3:]
    listed = outs[0].shape[0]
    total = squares[0][...]
    for part in squares[1:]:
        total = total + part[...]
    ids = [lax.broadcasted_iota(jnp.int32, total.shape, axis) for axis in range(2)]
    scale = jnp.where(ids[0] == ids[1], lax.rsqrt(total / D + EPSILON), 0.0)
    scale = jnp.sum(scale, axis=0, keepdims=True)
    scale = jnp.sum(pick[...] * scale, axis=1, keepdims=True)
    normed = residual[...] * scale * gain[...].astype(jnp.float32)[None, :]
    picked = normed.astype(jnp.bfloat16)
    place = 0
    for source in weights:
        for first in range(0, source.shape[1], CHUNK):
            product = jnp.dot(
                picked, source[:, first : first + CHUNK], preferred_element_type=jnp.float32
            )
            for shift in range(pool_count):
                outs[shift][:, place : place + CHUNK] = product[
                    shift * listed : (shift + 1) * listed
                ]
            place += CHUNK


def attend_kernel(
    pool_count, local_kv, group, routes, context_len, slot_route, slot_block, turn, *rest
):
    parts, (keys, values, out) = rest[:pool_count], rest[pool_count : pool_count + 3]
    turned, flat_query, flat_own, query, score, peak, mass, total = rest[pool_count + 3 :]
    listed = parts[0].shape[0]
    heads = local_kv * group
    slots = keys.shape[0]
    key_width = local_kv * HD
    homes = pool_count
    per_home = listed // homes
    score_scale = 1.0 / math.sqrt(HD)
    me = lax.axis_index("pool")
    for row in range(listed):
        turned[row : row + 1, :] = turn[pl.ds(listed_at(routes, me, row), 1), :]
    cosine, sine = turned[:, :HD], turned[:, HD:]

    def column(first):
        value = parts[1][:, first : first + HD]
        for part in parts[2:]:
            value = value + part[:, first : first + HD]
        return parts[0][:, first : first + HD] + value * (1.0 / GROW)

    def rotated(first):
        vector = column(first)
        vector = vector * cosine + pltpu.roll(vector, HD // 2, 1) * sine
        return vector.astype(jnp.bfloat16).astype(jnp.float32)

    new_keys = [rotated(k * HD) for k in range(local_kv)]
    new_values = [
        column(key_width + k * HD).astype(jnp.bfloat16).astype(jnp.float32)
        for k in range(local_kv)
    ]
    for head in range(heads):
        vector = rotated(2 * key_width + head * HD)
        own = jnp.sum(vector * new_keys[head // group], axis=1, keepdims=True) * score_scale
        flat_query[head * listed : (head + 1) * listed, :] = vector
        flat_own[head * listed : (head + 1) * listed, :] = jnp.broadcast_to(own, (listed, HD))
    lanes = lax.broadcasted_iota(jnp.int32, (heads, HD), 1)
    head_kv = lax.broadcasted_iota(jnp.int32, (heads, HD), 0) // group

    owns, mine = [], []
    peak[...] = jnp.full(peak.shape, NEG_FILL, jnp.float32)
    for row in range(listed):
        home = row // per_home
        request = listed_at(routes, me, row)
        taken = jnp.int32(0)
        for owner in range(pool_count):
            for place in range(per_home):
                same = routes[owner, place, home] == request
                taken = taken | ((owner < me) & same).astype(jnp.int32)
        vector = flat_query[pl.ds(row, heads, stride=listed), :]
        query[row] = jnp.concatenate(
            [jnp.where(head_kv == k, vector, 0.0) for k in range(local_kv)], axis=1
        ).astype(jnp.bfloat16)
        own = flat_own[pl.ds(row, heads, stride=listed), :]
        own = jnp.where(taken == 0, own, NEG_FILL)
        owns.append(own)
        mine.append(taken == 0)

    def slot_of(slot):
        entry = slot_route[slot]
        row = jnp.maximum(entry, 0)
        length = jnp.where(entry >= 0, context_len[listed_at(routes, me, row)], 0)
        return row, length - slot_block[slot] * BS

    for slot in range(slots):
        row, limit = slot_of(slot)
        value = (
            lax.dot_general(
                query[row],
                keys[slot],
                (((1,), (1,)), ((), ())),
                preferred_element_type=jnp.float32,
            )
            * score_scale
        )
        value = jnp.where(lanes < limit, value, NEG_FILL)
        score[slot] = value
        peak[row] = jnp.maximum(peak[row], value)
    for row in range(listed):
        top = jnp.maximum(jnp.max(peak[row], axis=1, keepdims=True), owns[row])
        peak[row] = top
        weight = jnp.where(mine[row], jnp.exp(owns[row] - top), 0.0)
        mass[row] = jnp.where(lanes == 0, weight, 0.0)
        fresh = jnp.zeros((heads, HD), jnp.float32)
        for k in range(local_kv):
            fresh = jnp.where(
                head_kv == k, jnp.broadcast_to(new_values[k][row : row + 1], (heads, HD)), fresh
            )
        total[row] = weight * fresh
    for slot in range(slots):
        row, limit = slot_of(slot)
        expo = jnp.where(lanes < limit, jnp.exp(score[slot] - peak[row]), 0.0)
        mass[row] += expo
        wide = jnp.dot(
            expo.astype(jnp.bfloat16), values[slot], preferred_element_type=jnp.float32
        )
        product = wide[:, :HD]
        for k in range(1, local_kv):
            product = jnp.where(head_kv == k, wide[:, k * HD : (k + 1) * HD], product)
        total[row] += product
    stats = jnp.zeros((heads, HD), jnp.float32)
    for row in range(listed):
        row_mass = jnp.sum(mass[row], axis=1, keepdims=True)
        row_peak = peak[row]
        out[row] = jnp.where(
            row_mass > 0.0, total[row] / jnp.where(row_mass > 0.0, row_mass, 1.0), 0.0
        ).astype(jnp.bfloat16)
        for first, left in ((0, row_peak), (3, row_mass)):
            for piece in range(first, first + 3):
                part = left.astype(jnp.bfloat16).astype(jnp.float32)
                stats = jnp.where(lanes == piece * listed + row, part, stats)
                left = left - part
    out[listed] = stats.astype(jnp.bfloat16)


def merge_kernel(pool_count, routes, *rest):
    parts, (w_out, out, flat) = rest[:pool_count], rest[pool_count:]
    listed = parts[0].shape[0] - 1
    heads = parts[0].shape[1]
    requests = out.shape[0]
    me = lax.axis_index("pool")
    flat[:, : requests * heads, :] = jnp.zeros((pool_count, requests * heads, HD), jnp.float32)
    lanes = lax.broadcasted_iota(jnp.int32, (heads, HD), 1)
    asked, there, peaks, masses = [], [], [], []
    for place, shift in enumerate([0, *shifts(pool_count)]):
        owner = lax.rem(me + pool_count - shift, pool_count)
        asked.append([listed_at(routes, owner, row) for row in range(listed)])
        stats = parts[place][listed].astype(jnp.float32)
        stats = (
            stats + pltpu.roll(stats, HD - listed, 1) + pltpu.roll(stats, HD - 2 * listed, 1)
        )
        source = jnp.full((heads, HD), -1, jnp.int32)
        for row, request in enumerate(asked[-1]):
            source = jnp.where(lanes == request, row, source)
        there.append(source >= 0)
        source = jnp.maximum(source, 0)
        peaks.append(
            jnp.where(there[-1], jnp.take_along_axis(stats, source, axis=1), NEG_FILL)
        )
        masses.append(jnp.take_along_axis(stats, source + 3 * listed, axis=1))
    best = functools.reduce(jnp.maximum, peaks)
    weights = [
        jnp.where(here, jnp.exp(peak - best) * mass, 0.0)
        for here, peak, mass in zip(there, peaks, masses)
    ]
    whole = sum(weights[1:], weights[0])
    whole = jnp.where(lanes < requests, whole, 1.0)
    for place, ids in enumerate(asked):
        back = jnp.zeros((heads, HD), jnp.int32)
        for row, request in enumerate(ids):
            back = jnp.where(lanes == row, request, back)
        weight = jnp.take_along_axis(weights[place] / whole, back, axis=1)
        for row, request in enumerate(ids):
            block = pl.ds(pl.multiple_of(request * heads, heads), heads)
            flat[place, block, :] = weight[:, row : row + 1] * parts[place][row].astype(
                jnp.float32
            )
    columns = []
    for head in range(heads):
        block = pl.ds(head, requests, stride=heads)
        value = flat[0, block, :]
        for place in range(1, pool_count):
            value = value + flat[place, block, :]
        columns.append(value.astype(jnp.bfloat16))
    attention = jnp.concatenate(columns, axis=1)
    for first in range(0, out.shape[1], CHUNK):
        out[:, first : first + CHUNK] = jnp.dot(
            attention, w_out[:, first : first + CHUNK], preferred_element_type=jnp.float32
        ).astype(jnp.bfloat16)


def shifts(pool_count):
    return range(1, pool_count)


def shifted(value, axis, shift):
    count = lax.axis_size(axis)
    return lax.ppermute(value, axis, [(i, (i + shift) % count) for i in range(count)])


def pin(value):
    return pltpu.with_memory_space_constraint(value, pltpu.VMEM)


def close_pool(
    residual,
    norm_gain,
    w_query,
    w_key,
    w_value,
    w_out,
    k_cache,
    v_cache,
    context_len,
    routes,
    slot_route,
    slot_block,
):
    pool_count = lax.axis_size("pool")
    requests, depth = residual.shape
    query_width, key_width = w_query.shape[1], w_key.shape[1]
    heads, local_kv = query_width // HD, key_width // HD
    group = heads // local_kv
    listed = routes.shape[1] * routes.shape[2]
    slots = k_cache.shape[0]
    width = query_width + 2 * key_width
    routes = routes.transpose(0, 2, 1)
    in_smem = pl.BlockSpec(memory_space=pltpu.SMEM)
    in_vmem = pl.BlockSpec(memory_space=pltpu.VMEM)
    f32 = jnp.float32
    spell = pl.CostEstimate(flops=2**34, bytes_accessed=2**25, transcendentals=0)

    squares = pl.pallas_call(
        square_kernel,
        out_shape=jax.ShapeDtypeStruct((requests, HD), f32),
        in_specs=[in_vmem],
        out_specs=in_vmem,
        compiler_params=pltpu.CompilerParams(vmem_limit_bytes=4 * 2**20),
        cost_estimate=spell,
        name="square",
    )(residual)
    rows = pool_count * listed
    picked, pick = pl.pallas_call(
        functools.partial(pick_kernel, pool_count, listed),
        out_shape=[
            jax.ShapeDtypeStruct((rows, depth), f32),
            jax.ShapeDtypeStruct((rows, HD), f32),
        ],
        in_specs=[in_smem, in_vmem, in_vmem],
        out_specs=[in_vmem] * 2,
        compiler_params=pltpu.CompilerParams(vmem_limit_bytes=4 * 2**20),
        cost_estimate=spell,
        name="pick",
    )(routes, residual, squares)
    sent = pl.pallas_call(
        functools.partial(project_kernel, pool_count),
        out_shape=[jax.ShapeDtypeStruct((listed, width), f32)] * pool_count,
        in_specs=[in_vmem] * (pool_count + 6),
        out_specs=[in_vmem] * pool_count,
        compiler_params=pltpu.CompilerParams(vmem_limit_bytes=8 * 2**20),
        cost_estimate=spell,
        name="project",
    )(
        picked,
        pick,
        norm_gain,
        squares,
        *[shifted(squares, "pool", shift) for shift in range(1, pool_count)],
        pin(w_key),
        pin(w_value),
        pin(w_query),
    )
    received = [sent[0]] + [
        shifted((sent[shift] * GROW).astype(jnp.float16), "pool", shift).astype(f32)
        for shift in shifts(pool_count)
    ]
    frequencies = THETA ** (-2.0 * jnp.arange(HD // 2, dtype=f32) / HD)
    late_len, _ = lax.optimization_barrier((context_len, sent[0]))
    angles = late_len.astype(f32)[:, None] * frequencies[None, :]
    cosine, sine = jnp.cos(angles), jnp.sin(angles)
    turn = jnp.concatenate([cosine, cosine, -sine, sine], axis=1)
    partial = pl.pallas_call(
        functools.partial(attend_kernel, pool_count, local_kv, group),
        out_shape=jax.ShapeDtypeStruct((listed + 1, heads, HD), jnp.bfloat16),
        in_specs=[in_smem] * 4 + [in_vmem] * (pool_count + 3),
        out_specs=in_vmem,
        scratch_shapes=[
            pltpu.VMEM((listed, 2 * HD), f32),
            pltpu.VMEM(((heads + 1) * listed, HD), f32),
            pltpu.VMEM(((heads + 1) * listed, HD), f32),
            pltpu.VMEM((listed, heads, key_width), jnp.bfloat16),
            pltpu.VMEM((slots, heads, HD), f32),
            pltpu.VMEM((listed, heads, HD), f32),
            pltpu.VMEM((listed, heads, HD), f32),
            pltpu.VMEM((listed, heads, HD), f32),
        ],
        compiler_params=pltpu.CompilerParams(vmem_limit_bytes=8 * 2**20),
        cost_estimate=spell,
        name="attend",
    )(routes, context_len, slot_route, slot_block, turn, *received, pin(k_cache), pin(v_cache))
    partials = [partial] + [shifted(partial, "pool", shift) for shift in shifts(pool_count)]

    product = pl.pallas_call(
        functools.partial(merge_kernel, pool_count),
        out_shape=jax.ShapeDtypeStruct((requests, w_out.shape[1]), jnp.bfloat16),
        in_specs=[in_smem] + [in_vmem] * (pool_count + 1),
        out_specs=in_vmem,
        scratch_shapes=[pltpu.VMEM((pool_count, (requests + 1) * heads, HD), f32)],
        compiler_params=pltpu.CompilerParams(vmem_limit_bytes=8 * 2**20),
        cost_estimate=spell,
        name="merge",
    )(routes, *partials, pin(w_out))
    tensor_count = lax.axis_size("tensor")
    one, two, three = [
        lax.ppermute(product, "tensor", [(i, i ^ d) for i in range(tensor_count)]).astype(f32)
        for d in (1, 2, 3)
    ]
    product = product.astype(f32)
    return (residual.astype(f32) + ((product + one) + (two + three))).astype(jnp.bfloat16)


def rotate(vectors, positions):
    half_dim = vectors.shape[-1] // 2
    frequencies = THETA ** (-2.0 * jnp.arange(half_dim, dtype=jnp.float32) / vectors.shape[-1])
    angles = positions.astype(jnp.float32)[:, None] * frequencies[None, :]
    cosine = jnp.cos(angles)[:, None, :]
    sine_part = jnp.sin(angles)[:, None, :]
    first_half = vectors[..., :half_dim]
    second_half = vectors[..., half_dim:]
    return jnp.concatenate(
        [
            first_half * cosine - second_half * sine_part,
            second_half * cosine + first_half * sine_part,
        ],
        axis=-1,
    )


def send_back(parts):
    return (
        lax.all_to_all(parts[0], "pool", split_axis=0, concat_axis=0, tiled=True),
        lax.all_to_all(parts[1], "pool", split_axis=0, concat_axis=0, tiled=True),
        lax.all_to_all(parts[2], "pool", split_axis=0, concat_axis=0, tiled=True),
    )


def wide_pool(
    residual,
    norm_gain,
    w_query,
    w_key,
    w_value,
    w_out,
    k_cache,
    v_cache,
    context_len,
    routes,
    slot_route,
    slot_block,
):
    pool_count = lax.axis_size("pool")
    pool_index = lax.axis_index("pool")
    request_count = residual.shape[0]
    per_home = request_count // pool_count
    home_first = pool_index * per_home
    query_width = w_query.shape[1]
    key_width = w_key.shape[1]
    local_heads = query_width // HD
    local_kv = key_width // HD
    group_size = local_heads // local_kv
    slot_count = k_cache.shape[0]
    score_scale = 1.0 / math.sqrt(HD)
    resid_f = residual.astype(jnp.float32)
    square_total = lax.psum(jnp.sum(resid_f * resid_f, axis=1), "pool")
    normed = (
        resid_f
        * lax.rsqrt(square_total / D + EPSILON)[:, None]
        * norm_gain.astype(jnp.float32)[None, :]
    ).astype(jnp.bfloat16)
    owner_routes = lax.dynamic_slice_in_dim(routes, pool_index, 1, 0)[0].reshape(-1)
    slot_request = jnp.where(slot_route >= 0, owner_routes[jnp.maximum(slot_route, 0)], -1)
    key_blocks = k_cache.reshape(slot_count, BS, local_kv, HD)
    value_blocks = v_cache.reshape(slot_count, BS, local_kv, HD)
    positions = slot_block[:, None] * BS + jnp.arange(BS, dtype=jnp.int32)[None, :]
    sent_ids = lax.dynamic_slice_in_dim(routes, pool_index, 1, 1)[:, 0, :]
    home_rows = lax.psum_scatter(
        jnp.concatenate(
            [
                jnp.dot(normed, w_query, preferred_element_type=jnp.float32),
                jnp.dot(normed, w_key, preferred_element_type=jnp.float32),
                jnp.dot(normed, w_value, preferred_element_type=jnp.float32),
            ],
            axis=1,
        ),
        "pool",
        scatter_dimension=0,
        tiled=True,
    )
    home_len = lax.dynamic_slice_in_dim(context_len, home_first, per_home, 0)
    row_total = home_rows.shape[0]
    query = rotate(home_rows[:, :query_width].reshape(row_total, local_heads, HD), home_len).astype(
        jnp.bfloat16
    )
    key_new = rotate(
        home_rows[:, query_width : query_width + key_width].reshape(row_total, local_kv, HD),
        home_len,
    ).astype(jnp.bfloat16)
    value_new = (
        home_rows[:, query_width + key_width :]
        .astype(jnp.bfloat16)
        .reshape(row_total, local_kv, HD)
    )
    home_query = query.reshape(row_total, query_width)
    sent_query = home_query[sent_ids - home_first]
    sent_info = jnp.stack([sent_ids, context_len[sent_ids]], axis=-1)
    rows_query = lax.all_to_all(sent_query, "pool", split_axis=0, concat_axis=0, tiled=True)
    rows_info = lax.all_to_all(sent_info, "pool", split_axis=0, concat_axis=0, tiled=True)
    home_total = rows_query.shape[0]
    item_total = rows_query.shape[1]
    flat_query = rows_query.reshape(home_total * item_total, query_width)
    flat_ids = rows_info[..., 0].reshape(-1)
    flat_len = rows_info[..., 1].reshape(-1)
    matches = slot_request[:, None] == flat_ids[None, :]
    slot_query = jnp.dot(
        matches.astype(jnp.bfloat16), flat_query, preferred_element_type=jnp.float32
    ).astype(jnp.bfloat16)
    grouped = slot_query.reshape(slot_count, local_kv, group_size, HD)
    slot_len = jnp.sum(jnp.where(matches, flat_len[None, :], 0), axis=1)
    present = jnp.any(matches, axis=1)
    in_range = present[:, None] & (positions < slot_len[:, None])
    valid_mask = in_range[:, None, None, :]
    scores = (
        jnp.einsum("skgd,sbkd->skgb", grouped, key_blocks, preferred_element_type=jnp.float32)
        * score_scale
    )
    block_peak = jnp.max(jnp.where(valid_mask, scores, NEG_FILL), axis=3)
    exponent = jnp.exp(jnp.where(valid_mask, scores - block_peak[..., None], NEG_FILL))
    weights = exponent.astype(jnp.bfloat16)
    block_sum = jnp.einsum(
        "skgb,sbkd->skgd", weights, value_blocks, preferred_element_type=jnp.float32
    )
    block_mass = jnp.sum(exponent, axis=3)
    hits = matches.T
    row_peak = jnp.max(jnp.where(hits[:, :, None, None], block_peak[None], NEG_FILL), axis=1)
    factor = jnp.where(hits[:, :, None, None], jnp.exp(block_peak[None] - row_peak[:, None]), 0.0)
    row_sum = jnp.einsum("rskg,skgd->rkgd", factor, block_sum, precision=EXACT)
    row_mass = jnp.einsum("rskg,skg->rkg", factor, block_mass, precision=EXACT)
    back_sum, back_peak, back_mass = send_back(
        (
            row_sum.reshape(home_total, item_total, query_width),
            row_peak.reshape(home_total, item_total, local_heads),
            row_mass.reshape(home_total, item_total, local_heads),
        )
    )
    local_ids = (sent_ids - home_first).reshape(-1)
    owned = local_ids[:, None] == jnp.arange(per_home, dtype=jnp.int32)[None, :]
    sum_rows = back_sum.reshape(-1, local_kv, group_size, HD)
    peak_rows = back_peak.reshape(-1, local_kv, group_size)
    mass_rows = back_mass.reshape(-1, local_kv, group_size)
    query_grid = home_query.reshape(per_home, local_kv, group_size, HD)
    own_score = (
        jnp.einsum("rkgd,rkd->rkg", query_grid, key_new, preferred_element_type=jnp.float32)
        * score_scale
    )
    overall = jnp.maximum(
        own_score, jnp.max(jnp.where(owned[:, :, None, None], peak_rows[:, None], NEG_FILL), axis=0)
    )
    merge_weight = jnp.where(
        owned[:, :, None, None], jnp.exp(peak_rows[:, None] - overall[None]), 0.0
    )
    own_weight = jnp.exp(own_score - overall)
    numerator = (
        jnp.einsum("prkg,pkgd->rkgd", merge_weight, sum_rows, precision=EXACT)
        + own_weight[..., None] * value_new.astype(jnp.float32)[:, :, None, :]
    )
    denominator = jnp.einsum("prkg,pkg->rkg", merge_weight, mass_rows, precision=EXACT) + own_weight
    attention = (
        (numerator / denominator[..., None]).astype(jnp.bfloat16).reshape(per_home, query_width)
    )
    partial_out = jnp.dot(
        lax.all_gather(attention, "pool", axis=0, tiled=True),
        w_out,
        preferred_element_type=jnp.float32,
    )
    head_total = lax.psum(partial_out, "tensor")
    return (resid_f + head_total).astype(jnp.bfloat16)


def solution(mesh):
    placed = (
        P("groups", "pool"),
        P("pool"),
        P("pool", "tensor"),
        P("pool", "tensor"),
        P("pool", "tensor"),
        P("tensor", "pool"),
        P(("groups", "pool"), None, "tensor"),
        P(("groups", "pool"), None, "tensor"),
        P("groups"),
        P("groups", None, None),
        P(("groups", "pool")),
        P(("groups", "pool")),
    )
    pool_count, tensor_count = mesh.shape["pool"], mesh.shape["tensor"]
    close = pool_count <= 4 and tensor_count == 4
    return jax.shard_map(
        close_pool if close else wide_pool,
        mesh=mesh,
        in_specs=placed,
        out_specs=P("groups", "pool"),
        check_vma=False,
    )
```
